256 devices in a mesh: pool: 64 (over z, x, core), blk: 4 (over y).
Axes of the slice: x: 4, y: 4, z: 8, core: 2. Of those that a mesh axis runs over, the one named last changes fastest.
Arguments:
- query_emb: bfloat16 [65536, 512], P(('pool', 'blk')), may hold values from -5.4 to 5.4
- item_table: bfloat16 [131072, 1024], P(('pool', 'blk')), may hold values from -24 to 24
- w_in: bfloat16 [1024, 3072], replicated, may hold values from -0.1875 to 0.1875
- bias_in: float32 [3072], replicated, may hold values from -3 to 3
- w_out: bfloat16 [3072, 512], replicated, may hold values from -0.109375 to 0.109375
- fetch_rows: int32 [16384, 16], P(('pool', 'blk')), may hold values from 0 to 511, as said below
- fetch_counts: int32 [256, 64], P(('pool', 'blk')), may hold values from 0 to 16, as said below
- pos_slot: int32 [65536], P(('pool', 'blk')), may hold values from 0 to 511
Outputs:
- query_loss: float32 [65536], P(('pool', 'blk'))
- query_grad: float32 [65536, 512], P(('pool', 'blk'))
- table_grad: float32 [131072, 1024], P(('pool', 'blk'))
The draws below stay inside these ranges and needn't reach their ends.
Inputs may be any that keep to these rules, and one draw needn't show every extreme that they name: `fetch_rows`: the first fetch_counts[d, o] slots of a row name distinct rows of the shard; later slots are in range and ask for nothing. `fetch_counts`: each device's counts sum to exactly 512. In every draw each blk slice has one shard to which every device of the slice sends exactly 16 rows. `pos_slot`: several queries of a device may share one positive.
All inputs are finite; a program needn't handle non-finite values.
Results may differ from the reference program's by a relative error of at most 0.01825.
Values may be sent and summed in bfloat16 or wider, within the bound.
A program may use at most 128 MiB of HBM per device.

```python
import math
import jax
import jax.numpy as jnp
from jax import lax

F = 1024
HID = 3072
E = 512
ROWS_DEV = 512
POOL_DEV = 512
QRY_DEV = 256
CAP = 16
QUERIES = 65536
ITEMS = 131072
N_POOL = 64
N_BLK = 4
DEVICES = 256


def draw_query_emb(key, part):
    key = jax.random.fold_in(key, 11)
    row_key, col_key, base_key = jax.random.split(key, 3)
    row_scale = jnp.exp(jax.random.uniform(row_key, (QUERIES, 1), jnp.float32, math.log(0.03), math.log(0.3)))
    col_scale = jnp.exp(jax.random.uniform(col_key, (1, E), jnp.float32, math.log(0.3), math.log(3.0)))
    base_draw = jnp.clip(jax.random.normal(base_key, (QUERIES, E), jnp.float32), -6.0, 6.0)
    return (base_draw * row_scale * col_scale).astype(jnp.bfloat16)


def draw_item_table(key, part):
    key = jax.random.fold_in(key, 17)
    row_key, col_key, base_key = jax.random.split(key, 3)
    row_scale = jnp.exp(jax.random.uniform(row_key, (ITEMS, 1), jnp.float32, math.log(0.3), math.log(3.0)))
    col_scale = jnp.exp(jax.random.uniform(col_key, (1, F), jnp.float32, math.log(0.5), math.log(2.0)))
    base_draw = jnp.clip(jax.random.normal(base_key, (ITEMS, F), jnp.float32), -4.0, 4.0)
    return (base_draw * row_scale * col_scale).astype(jnp.bfloat16)


def draw_fetch_counts(key, part):
    key = jax.random.fold_in(key, 21)
    hot_key, perm_key, amount_key = jax.random.split(key, 3)
    half_cap = CAP // 2
    device_ids = jnp.arange(DEVICES, dtype=jnp.int32)
    hot_shard = jax.random.randint(hot_key, (N_BLK,), 0, N_POOL)
    hot_dev = jnp.take(hot_shard, device_ids % N_BLK)
    perms = jax.vmap(lambda one_key: jax.random.permutation(one_key, N_POOL))(jax.random.split(perm_key, DEVICES)).astype(jnp.int32)
    found_at = jnp.argmax((perms == hot_dev[:, None]).astype(jnp.int32), axis=1)
    leading = perms[:, 0]
    perms = perms.at[device_ids, found_at].set(leading)
    perms = perms.at[:, 0].set(hot_dev)
    amounts = jax.random.randint(amount_key, (DEVICES, N_POOL // 2), -half_cap, half_cap + 1)
    amounts = amounts.at[:, 0].set(half_cap)
    paired = jnp.stack([amounts, -amounts], axis=2).reshape(DEVICES, N_POOL)
    counts = jnp.zeros((DEVICES, N_POOL), jnp.int32).at[device_ids[:, None], perms].set(half_cap + paired)
    return counts.astype(jnp.int32)


def draw_fetch_rows(key, part):
    key = jax.random.fold_in(key, 33)
    first_key, second_key, stride_key = jax.random.split(key, 3)
    list_count = DEVICES * N_POOL
    first_pick = jax.random.randint(first_key, (list_count, 1), 0, POOL_DEV)
    second_pick = jax.random.randint(second_key, (list_count, 1), 0, POOL_DEV)
    start_row = first_pick * second_pick // POOL_DEV
    stride = 2 * jax.random.randint(stride_key, (list_count, 1), 0, POOL_DEV // 2) + 1
    slot_index = jnp.arange(CAP, dtype=jnp.int32)[None, :]
    return ((start_row + slot_index * stride) % POOL_DEV).astype(jnp.int32)


def touch_ends(result, rng, low, high):
    place = [jax.random.randint(jax.random.fold_in(rng, axis), (), 0, length) for axis, length in enumerate(result.shape)]
    longest = result.shape.index(max(result.shape))
    neighbour = place[:longest] + [(place[longest] + 1) % result.shape[longest]] + place[longest + 1:]
    return result.at[tuple(place)].set(low).at[tuple(neighbour)].set(high)


def bell_draw(own_key, shape, spread, bound, kind=jnp.bfloat16):
    array = jax.random.normal(own_key, shape, jnp.float32) * spread
    return jnp.minimum(jnp.maximum(array, -bound), bound).astype(kind)


def setup_inputs(seed: int = 0) -> dict:
    key_list = jax.random.split(jax.random.key(seed), 9)
    return {
        "query_emb": draw_query_emb(jax.random.fold_in(key_list[8], 71), 0),
        "item_table": draw_item_table(jax.random.fold_in(key_list[8], 71), 0),
        "w_in": bell_draw(key_list[2], (F, HID), F ** -0.5, 0.1875),
        "bias_in": bell_draw(key_list[3], (HID,), 0.5, 3.0, jnp.float32),
        "w_out": bell_draw(key_list[4], (HID, E), HID ** -0.5, 0.109375),
        "fetch_rows": draw_fetch_rows(jax.random.fold_in(key_list[8], 71), 0),
        "fetch_counts": draw_fetch_counts(jax.random.fold_in(key_list[8], 71), 0),
        "pos_slot": touch_ends(jax.random.randint(key_list[7], (QUERIES,), 0, ROWS_DEV), jax.random.fold_in(key_list[7], 1), 0, ROWS_DEV - 1).astype(jnp.int32),
    }


logit_scale = 80.0
norm_eps = 1e-06

def live_order(counts, live_total, capacity):
    count_ends = jnp.cumsum(counts)
    count_starts = count_ends - counts
    position = jnp.arange(live_total, dtype=jnp.int32)
    owner_of = lax.optimization_barrier(jnp.sum((count_ends[None, :] <= position[:, None]).astype(jnp.int32), axis=1))
    within_slot = position - jnp.take(count_starts, owner_of)
    return (owner_of * capacity + within_slot).astype(jnp.int32)

def reference(query_emb, item_table, w_in, bias_in, w_out, fetch_rows, fetch_counts, pos_slot):
    rows_all = fetch_rows.reshape(N_POOL, N_BLK, N_POOL, CAP)
    counts_all = fetch_counts.reshape(N_POOL, N_BLK, N_POOL)
    query_all = query_emb.reshape(N_POOL, N_BLK * QRY_DEV, E)
    target_all = pos_slot.reshape(N_POOL, N_BLK, QRY_DEV)
    slice_ids = jnp.arange(N_BLK, dtype=jnp.int32)
    owner_ids = jnp.arange(N_POOL, dtype=jnp.int32)

    def request_ids(rows_dev, counts_dev, blk_id):
        slot_of = live_order(counts_dev, ROWS_DEV, CAP)
        shard_rows = (owner_ids[:, None] * N_BLK + blk_id) * POOL_DEV + rows_dev
        return jnp.take(shard_rows.reshape(-1), slot_of).astype(jnp.int32)

    def one_group(inputs):
        rows_grp, counts_grp, query_grp, target_grp = inputs
        item_ids = jax.vmap(request_ids)(rows_grp, counts_grp, slice_ids).reshape(-1)
        features = jnp.take(item_table, item_ids, axis=0)
        pre_act = jnp.dot(features, w_in, preferred_element_type=jnp.float32) + bias_in
        hidden = jax.nn.silu(pre_act).astype(jnp.bfloat16)
        tower_out = jnp.dot(hidden, w_out, preferred_element_type=jnp.float32)
        item_inv = lax.rsqrt(lax.optimization_barrier(jnp.sum(tower_out * tower_out, axis=1, keepdims=True)) + norm_eps)
        item_vec = (tower_out * item_inv).astype(jnp.bfloat16)
        query_f = query_grp.astype(jnp.float32)
        query_inv = lax.rsqrt(lax.optimization_barrier(jnp.sum(query_f * query_f, axis=1, keepdims=True)) + norm_eps)
        query_vec = (query_f * query_inv).astype(jnp.bfloat16)
        scores = logit_scale * lax.dot_general(query_vec, item_vec, (((1,), (1,)), ((), ())), preferred_element_type=jnp.float32)
        totals = jnp.log(lax.optimization_barrier(jnp.sum(jnp.exp(scores), axis=1)))
        targets = (slice_ids[:, None] * ROWS_DEV + target_grp).reshape(-1).astype(jnp.int32)
        picked = jnp.take_along_axis(scores, targets[:, None], axis=1)[:, 0]
        columns = jnp.arange(N_BLK * ROWS_DEV, dtype=jnp.int32)
        target_hit = (columns[None, :] == targets[:, None]).astype(jnp.float32)
        grad_coef = (jnp.exp(scores - totals[:, None]) - target_hit).astype(jnp.bfloat16)
        vec_grad = logit_scale * jnp.dot(grad_coef, item_vec, preferred_element_type=jnp.float32)
        query_grad = vec_grad * query_inv - query_f * query_inv ** 3 * lax.optimization_barrier(jnp.sum(query_f * vec_grad, axis=1, keepdims=True))
        item_grad = logit_scale * lax.dot_general(grad_coef, query_vec, (((0,), (0,)), ((), ())), preferred_element_type=jnp.float32)
        tower_grad = (item_grad * item_inv - tower_out * item_inv ** 3 * lax.optimization_barrier(jnp.sum(tower_out * item_grad, axis=1, keepdims=True))).astype(jnp.bfloat16)
        hidden_grad = lax.dot_general(tower_grad, w_out, (((1,), (1,)), ((), ())), preferred_element_type=jnp.float32)
        gate_sig = jax.nn.sigmoid(pre_act)
        pre_grad = (hidden_grad * gate_sig * (1.0 + pre_act * (1.0 - gate_sig))).astype(jnp.bfloat16)
        feats_grad = lax.dot_general(pre_grad, w_in, (((1,), (1,)), ((), ())), preferred_element_type=jnp.float32)
        return (totals - picked, query_grad, feats_grad, item_ids)
    losses, query_grads, feats_grads, all_ids = lax.map(one_group, (rows_all, counts_all, query_all, target_all))
    table_grad = jax.ops.segment_sum(feats_grads.reshape(-1, F), all_ids.reshape(-1), num_segments=ITEMS)
    return (losses.reshape(-1), query_grads.reshape(-1, E), table_grad)
```

```python
import jax
import jax.numpy as jnp
from jax import lax
from jax.sharding import PartitionSpec as P

logit_scale = 80.0
norm_eps = 1e-06


def on_device(query_emb, item_table, w_in, bias_in, w_out, fetch_rows, fetch_counts, pos_slot):
    owners = lax.axis_size("pool")
    blks = lax.axis_size("blk")
    capacity = fetch_rows.shape[1]
    slots = owners * capacity
    pool_rows = item_table.shape[0]
    queries = query_emb.shape[0]
    own = lax.axis_index("blk")

    query_f = query_emb.astype(jnp.float32)
    query_inv = lax.rsqrt(jnp.sum(query_f * query_f, axis=1, keepdims=True) + norm_eps)
    query_vec = (query_f * query_inv).astype(jnp.bfloat16)
    group_vec = lax.all_gather(query_vec, "blk", axis=0, tiled=True)

    asked = lax.all_to_all(fetch_rows, "pool", split_axis=0, concat_axis=0, tiled=True)
    pre_act = jnp.dot(item_table, w_in, preferred_element_type=jnp.float32) + bias_in
    hidden = jax.nn.silu(pre_act).astype(jnp.bfloat16)
    tower_out = jnp.dot(hidden, w_out, preferred_element_type=jnp.float32)
    item_inv = lax.rsqrt(jnp.sum(tower_out * tower_out, axis=1, keepdims=True) + norm_eps)
    item_vec = (tower_out * item_inv).astype(jnp.bfloat16)

    pick = (asked.reshape(slots, 1) == jnp.arange(pool_rows, dtype=jnp.int32)[None, :]).astype(jnp.bfloat16)
    served = jnp.dot(pick, item_vec, preferred_element_type=jnp.float32).astype(jnp.bfloat16)
    arrived = lax.all_to_all(
        served.reshape(owners, capacity, -1), "pool", split_axis=0, concat_axis=0, tiled=True
    ).reshape(slots, -1)

    counts = fetch_counts[0]
    ends = jnp.cumsum(counts)
    slot_column = jnp.arange(capacity, dtype=jnp.int32)
    live = (slot_column[None, :] < counts[:, None]).reshape(slots, 1)
    past = (ends[:, None] <= pos_slot[None, :]).astype(jnp.int32)
    target = jnp.sum(past * (capacity - counts[:, None]), axis=0) + pos_slot
    target = jnp.where(
        (jnp.arange(blks, dtype=jnp.int32) == own)[:, None], target[None, :], -1
    ).reshape(-1)
    hit = jnp.arange(slots, dtype=jnp.int32)[:, None] == target[None, :]

    scores = logit_scale * lax.dot_general(
        arrived, group_vec, (((1,), (1,)), ((), ())), preferred_element_type=jnp.float32
    )
    sums = jnp.sum(jnp.where(live, jnp.exp(scores), 0.0), axis=0)
    picked = jnp.sum(jnp.where(hit, scores, 0.0), axis=0)
    parts = [sums]
    for shift in range(1, blks):
        perm = [(i, (i + shift) % blks) for i in range(blks)]
        parts.append(lax.ppermute(sums, "blk", perm))
    totals = jnp.log(sum(parts[1:], parts[0]))
    mine = lax.dynamic_slice(totals - picked, (own * queries,), (queries,))
    coef = (
        jnp.where(live, jnp.exp(scores - totals[None, :]), 0.0) - hit.astype(jnp.float32)
    ).astype(jnp.bfloat16)
    item_grad = (
        logit_scale * jnp.dot(coef, group_vec, preferred_element_type=jnp.float32)
    ).astype(jnp.bfloat16)
    returned = lax.all_to_all(
        item_grad.reshape(owners, capacity, -1), "pool", split_axis=0, concat_axis=0, tiled=True
    ).reshape(slots, -1)

    part_grad = logit_scale * lax.dot_general(
        coef, arrived, (((0,), (0,)), ((), ())), preferred_element_type=jnp.float32
    )
    vec_grad = lax.psum_scatter(
        part_grad.astype(jnp.bfloat16), "blk", scatter_dimension=0, tiled=True
    ).astype(jnp.float32)
    query_grad = vec_grad * query_inv - query_f * query_inv**3 * jnp.sum(
        query_f * vec_grad, axis=1, keepdims=True
    )

    row_grad = lax.dot_general(
        pick, returned, (((0,), (0,)), ((), ())), preferred_element_type=jnp.float32
    )
    tower_grad = (
        row_grad * item_inv
        - tower_out * item_inv**3 * jnp.sum(tower_out * row_grad, axis=1, keepdims=True)
    ).astype(jnp.bfloat16)
    hidden_grad = lax.dot_general(
        tower_grad, w_out, (((1,), (1,)), ((), ())), preferred_element_type=jnp.float32
    )
    gate_sig = jax.nn.sigmoid(pre_act)
    pre_grad = (hidden_grad * gate_sig * (1.0 + pre_act * (1.0 - gate_sig))).astype(jnp.bfloat16)
    table_grad = lax.dot_general(
        pre_grad, w_in, (((1,), (1,)), ((), ())), preferred_element_type=jnp.float32
    )
    return (mine, query_grad, table_grad)


def solution(mesh):
    placed = (
        P(("pool", "blk"), None),
        P(("pool", "blk"), None),
        P(),
        P(),
        P(),
        P(("pool", "blk"), None),
        P(("pool", "blk"), None),
        P(("pool", "blk")),
    )
    return jax.shard_map(
        on_device,
        mesh=mesh,
        in_specs=placed,
        out_specs=(P(("pool", "blk")), P(("pool", "blk"), None), P(("pool", "blk"), None)),
        check_vma=False,
    )
```

```python
import functools

import jax
import jax.numpy as jnp
from jax import lax
from jax.experimental import pallas as pl
from jax.experimental.pallas import tpu as pltpu
from jax.sharding import PartitionSpec as P

logit_scale = 80.0
norm_eps = 1e-06
shift = 2.772588722239781

MESH = pl.DeviceIdType.MESH
f32 = jnp.float32
bf16 = jnp.bfloat16
NN = (((1,), (0,)), ((), ()))
NT = (((1,), (1,)), ((), ()))
TN = (((0,), (0,)), ((), ()))


def mm(a, b, dims=NN):
    return lax.dot_general(a, b, dims, preferred_element_type=f32)


def iota(shape, dim):
    return lax.broadcasted_iota(jnp.int32, shape, dim)


def step_kernel(
    n, nb, group,
    query_ref, table_hbm, win_hbm, bias_ref, wout_hbm, rows_ref, counts_ref, pos_ref,
    loss_ref, qgrad_ref, tgrad_hbm,
    table, win, wout, dsilu, tower, item_vec, idx_send, idx_recv, idx_flat, idx_col, idx_row,
    serve, arrive, group_vec, live_col, expo, coef, sums, lossbuf, grad, ret, vg_send, vg_recv,
    row_grad, pre_grad, out_buf,
    w_sem, o_sem, isend, irecv, fsend, frecv, bsend, brecv, qsend, qrecv, ssend, srecv, vsend, vrecv,
):
    p = lax.axis_index("pool")
    b = lax.axis_index("blk")
    cap = rows_ref.shape[1]
    slots = n * cap
    span = group * cap
    groups = n // group
    queries, width = query_ref.shape
    chunks, feats, chunk = win.shape
    pool_rows = table.shape[0]
    outs, out_cols = out_buf.shape[0], out_buf.shape[2]

    def load_table():
        return pltpu.make_async_copy(table_hbm, table, w_sem.at[2 * chunks])

    def load_win(c):
        return pltpu.make_async_copy(
            win_hbm.at[:, pl.ds(pl.multiple_of(c * chunk, chunk), chunk)], win.at[c], w_sem.at[c]
        )

    def load_wout(c):
        return pltpu.make_async_copy(
            wout_hbm.at[pl.ds(pl.multiple_of(c * chunk, chunk), chunk), :],
            wout.at[c],
            w_sem.at[chunks + c],
        )

    def ahead(k):
        return lax.rem(p + k, n)

    def behind(k):
        return lax.rem(p + n - k, n)

    def idx_copy(k):
        return pltpu.make_async_remote_copy(
            src_ref=idx_send.at[k], dst_ref=idx_recv.at[k], send_sem=isend.at[k],
            recv_sem=irecv.at[k], device_id={"pool": ahead(k)}, device_id_type=MESH,
        )

    def rows_of(k):
        return pl.ds(pl.multiple_of(k * cap, cap), cap)

    def fwd_copy(k):
        return pltpu.make_async_remote_copy(
            src_ref=serve.at[rows_of(k)], dst_ref=arrive.at[rows_of(k)], send_sem=fsend.at[k],
            recv_sem=frecv.at[k], device_id={"pool": behind(k)}, device_id_type=MESH,
        )

    def bwd_copy(k):
        return pltpu.make_async_remote_copy(
            src_ref=grad.at[rows_of(k)], dst_ref=ret.at[rows_of(k)], send_sem=bsend.at[k],
            recv_sem=brecv.at[k], device_id={"pool": ahead(k)}, device_id_type=MESH,
        )

    def block_of(c):
        return pl.ds(pl.multiple_of(c * queries, queries), queries)

    def query_copy(j):
        return pltpu.make_async_remote_copy(
            src_ref=group_vec.at[block_of(b)], dst_ref=group_vec.at[block_of(b)],
            send_sem=qsend.at[j], recv_sem=qrecv.at[j],
            device_id={"blk": lax.rem(b + j, nb)}, device_id_type=MESH,
        )

    def query_arrival(j):
        src = lax.rem(b + nb - j, nb)
        return pltpu.make_async_remote_copy(
            src_ref=group_vec.at[block_of(src)], dst_ref=group_vec.at[block_of(src)],
            send_sem=qsend.at[j], recv_sem=qrecv.at[j],
            device_id={"blk": lax.rem(b + j, nb)}, device_id_type=MESH,
        )

    def sums_copy(j):
        return pltpu.make_async_remote_copy(
            src_ref=sums.at[b], dst_ref=sums.at[b], send_sem=ssend.at[j], recv_sem=srecv.at[j],
            device_id={"blk": lax.rem(b + j, nb)}, device_id_type=MESH,
        )

    def sums_arrival(j):
        src = lax.rem(b + nb - j, nb)
        return pltpu.make_async_remote_copy(
            src_ref=sums.at[src], dst_ref=sums.at[src], send_sem=ssend.at[j],
            recv_sem=srecv.at[j],
            device_id={"blk": lax.rem(b + j, nb)}, device_id_type=MESH,
        )

    def vg_copy(j):
        return pltpu.make_async_remote_copy(
            src_ref=vg_send.at[j], dst_ref=vg_recv.at[j], send_sem=vsend.at[j],
            recv_sem=vrecv.at[j],
            device_id={"blk": lax.rem(b + j, nb)}, device_id_type=MESH,
        )

    def loop(low, high, body):
        lax.fori_loop(low, high, lambda k, _: (body(k), 0)[1], 0)

    load_table().start()
    loop(0, chunks, lambda c: (load_win(c).start(), load_wout(c).start()))
    barrier = pltpu.get_barrier_semaphore()

    def greet(k):
        pl.semaphore_signal(barrier, inc=1, device_id={"pool": ahead(k)}, device_id_type=MESH)

    def greet_blk(j):
        pl.semaphore_signal(
            barrier, inc=1, device_id={"blk": lax.rem(b + j, nb)}, device_id_type=MESH
        )

    loop(1, n, greet)
    loop(1, nb, greet_blk)

    query_f = query_ref[...].astype(f32)
    query_inv = lax.rsqrt(jnp.sum(query_f * query_f, axis=1, keepdims=True) + norm_eps)
    group_vec[block_of(b), :] = (query_f * query_inv).astype(bf16)

    idx_send[...] = jnp.zeros_like(idx_send)

    def put_rows(k):
        idx_send[k, :, 0:cap] = rows_ref[pl.ds(ahead(k), 1), :]

    loop(0, n, put_rows)

    counts = counts_ref[...].astype(f32)
    slot_owner = lax.rem(iota((slots, n), 0) // cap + p, n)
    slot_count = jnp.sum(
        jnp.where(slot_owner == iota((slots, n), 1), counts, 0.0), axis=1, keepdims=True
    )
    live_col[...] = (
        lax.rem(iota((slots, 1), 0), cap).astype(f32) < slot_count
    ).astype(f32)
    own_order = iota((n, n), 0)
    other = iota((n, n), 1)
    ends = jnp.sum(jnp.where(other <= own_order, counts, 0.0), axis=1, keepdims=True)
    count_col = jnp.sum(jnp.where(other == own_order, counts, 0.0), axis=1, keepdims=True)
    pos = pos_ref[...].astype(f32)
    past = ends <= pos
    owner = jnp.sum(jnp.where(past, 1.0, 0.0), axis=0, keepdims=True)
    start = jnp.sum(jnp.where(past, count_col, 0.0), axis=0, keepdims=True)
    owner_rel = lax.rem(owner.astype(jnp.int32) + (n - p), n)
    target = owner_rel * cap + (pos - start).astype(jnp.int32)
    target_all = jnp.concatenate([target] * nb, axis=1)
    target_all = jnp.where(iota((1, nb * queries), 1) // queries == b, target_all, -1)

    def tower_chunk(c):
        load_win(c).wait()
        load_wout(c).wait()
        cols = pl.ds(pl.multiple_of(c * chunk, chunk), chunk)
        pre = mm(table[...], win[c]) + bias_ref[:, cols]
        sig = 1.0 / (1.0 + jnp.exp(-pre))
        act = pre * sig
        dsilu[c] = (sig * (1.0 + pre - act)).astype(bf16)
        tower[...] += mm(act.astype(bf16), wout[c])

    tower[...] = jnp.zeros_like(tower)
    load_table().wait()
    early = max(1, chunks // 3)
    loop(0, early, tower_chunk)

    pl.semaphore_wait(barrier, n + nb - 2)
    loop(1, n, lambda k: idx_copy(k).start())
    loop(1, nb, lambda j: query_copy(j).start())
    idx_recv[0] = idx_send[0]
    loop(early, chunks, tower_chunk)

    tower_out = tower[...]
    item_inv = lax.rsqrt(jnp.sum(tower_out * tower_out, axis=1, keepdims=True) + norm_eps)
    item_vec[...] = (tower_out * item_inv).astype(bf16)

    loop(1, n, lambda k: idx_copy(k).wait_recv())

    def flat(k):
        idx_flat[pl.ds(k, 1), :] = idx_recv[k]

    loop(0, n, flat)
    low = lax.rem(idx_flat[...], 16)
    high = (idx_flat[...] - low).astype(f32).astype(bf16)
    low = low.astype(f32).astype(bf16)
    lanes = idx_flat.shape[1]
    spread = (iota((slots, n), 0) // cap == iota((slots, n), 1)).astype(f32).astype(bf16)
    wide = mm(spread, high) + mm(spread, low)
    idx_col[...] = jnp.sum(
        jnp.where(iota((slots, lanes), 1) == lax.rem(iota((slots, lanes), 0), cap), wide, 0.0),
        axis=1, keepdims=True,
    )
    spread_t = (iota((n, slots), 1) // cap == iota((n, slots), 0)).astype(f32).astype(bf16)
    tall = mm(high, spread_t, TN) + mm(low, spread_t, TN)
    idx_row[...] = jnp.sum(
        jnp.where(iota((lanes, slots), 0) == lax.rem(iota((lanes, slots), 1), cap), tall, 0.0),
        axis=0, keepdims=True,
    )

    def span_of(g):
        return pl.ds(pl.multiple_of(g * span, span), span)

    def serve_group(g):
        pick = (
            idx_col[span_of(g), :] == iota((span, pool_rows), 1).astype(f32)
        ).astype(f32).astype(bf16)
        serve[span_of(g), :] = mm(pick, item_vec[...]).astype(bf16)

        def send(i):
            k = g * group + i

            @pl.when(k > 0)
            def _():
                fwd_copy(k).start()

        loop(0, group, send)

    loop(0, groups, serve_group)
    arrive[rows_of(0), :] = serve[rows_of(0), :]

    loop(1, nb, lambda j: query_arrival(j).wait_recv())
    all_queries = nb * queries
    sums[b] = jnp.zeros((1, all_queries), f32)
    lossbuf[...] = jnp.zeros_like(lossbuf)

    def hits(g):
        return iota((span, all_queries), 0) + g * span == target_all

    def score_group(g):
        def arrival(i):
            k = g * group + i

            @pl.when(k > 0)
            def _():
                fwd_copy(k).wait_recv()

        loop(0, group, arrival)
        scores = logit_scale * mm(arrive[span_of(g), :], group_vec[...], NT)
        part = jnp.exp(scores - shift) * live_col[span_of(g), :]
        expo[span_of(g), :] = part
        sums[b] = sums[b] + jnp.sum(part, axis=0, keepdims=True)
        lossbuf[...] += jnp.sum(jnp.where(hits(g), scores, 0.0), axis=0, keepdims=True)

    loop(0, groups, score_group)
    loop(1, nb, lambda j: sums_copy(j).start())
    loop(1, nb, lambda j: sums_arrival(j).wait_recv())
    total = sums[0]
    for j in range(1, nb):
        total = total + sums[j]
    inv_total = 1.0 / total
    lossbuf[...] = jnp.log(total) + shift - lossbuf[...]
    loss_ref[...] = lossbuf[:, block_of(b)]

    def coef_group(g):
        part = expo[span_of(g), :] * inv_total - jnp.where(hits(g), 1.0, 0.0)
        part = part.astype(bf16)
        coef[span_of(g), :] = part
        grad[span_of(g), :] = (logit_scale * mm(part, group_vec[...])).astype(bf16)

        def send(i):
            k = g * group + i

            @pl.when(k > 0)
            def _():
                bwd_copy(k).start()

        loop(0, group, send)

    loop(0, groups, coef_group)
    ret[rows_of(0), :] = grad[rows_of(0), :]

    def part_of(c):
        return logit_scale * mm(coef[:, block_of(c)], arrive[...], TN)

    def send_part(j):
        vg_send[j] = part_of(lax.rem(b + j, nb)).astype(bf16)
        vg_copy(j).start()

    loop(1, nb, send_part)
    vec_grad = part_of(b)

    row_grad[...] = jnp.zeros_like(row_grad)

    def sum_group(g):
        def arrival(i):
            k = g * group + i

            @pl.when(k > 0)
            def _():
                bwd_copy(k).wait_recv()

        loop(0, group, arrival)
        pick_t = (
            iota((pool_rows, span), 0).astype(f32) == idx_row[:, span_of(g)]
        ).astype(f32).astype(bf16)
        row_grad[...] += mm(pick_t, ret[span_of(g), :])

    loop(0, groups // 2, sum_group)
    loop(1, nb, lambda j: vg_copy(j).wait_recv())
    for j in range(1, nb):
        vec_grad = vec_grad + vg_recv[j].astype(f32)
    query_f = query_ref[...].astype(f32)
    qgrad_ref[...] = vec_grad * query_inv - query_f * (query_inv * query_inv * query_inv) * jnp.sum(
        query_f * vec_grad, axis=1, keepdims=True
    )
    loop(groups // 2, groups, sum_group)

    tower_out = tower[...]
    item_inv = lax.rsqrt(jnp.sum(tower_out * tower_out, axis=1, keepdims=True) + norm_eps)
    summed = row_grad[...]
    item_vec[...] = (
        summed * item_inv
        - tower_out * (item_inv * item_inv * item_inv)
        * jnp.sum(tower_out * summed, axis=1, keepdims=True)
    ).astype(bf16)

    def back_chunk(c):
        pre_grad[c] = (mm(item_vec[...], wout[c], NT) * dsilu[c].astype(f32)).astype(bf16)

    loop(0, chunks, back_chunk)

    def out_copy(f):
        return pltpu.make_async_copy(
            out_buf.at[f],
            tgrad_hbm.at[:, pl.ds(pl.multiple_of(f * out_cols, out_cols), out_cols)],
            o_sem.at[f],
        )

    def out_block(f):
        rows = pl.ds(pl.multiple_of(f * out_cols, out_cols), out_cols)
        total = mm(pre_grad[0], win[0, rows, :], NT)
        for c in range(1, chunks):
            total = total + mm(pre_grad[c], win[c, rows, :], NT)
        out_buf[f] = total
        out_copy(f).start()

    loop(0, outs, out_block)

    loop(1, n, lambda k: (idx_copy(k).wait_send(), fwd_copy(k).wait_send(), bwd_copy(k).wait_send()))
    loop(
        1, nb,
        lambda j: (query_copy(j).wait_send(), sums_copy(j).wait_send(), vg_copy(j).wait_send()),
    )
    loop(0, outs, lambda f: out_copy(f).wait())


def on_device(query_emb, item_table, w_in, bias_in, w_out, fetch_rows, fetch_counts, pos_slot):
    n = lax.axis_size("pool")
    nb = lax.axis_size("blk")
    cap = fetch_rows.shape[1]
    slots = n * cap
    queries, width = query_emb.shape
    pool_rows, feats = item_table.shape
    hid = w_in.shape[1]
    chunk = min(512, hid)
    chunks = hid // chunk
    group = min(16, n // 2)
    out_cols = min(256, feats)
    outs = feats // out_cols
    every = nb * queries
    in_vmem = pl.BlockSpec(memory_space=pltpu.VMEM)
    in_any = pl.BlockSpec(memory_space=pl.ANY)
    dma = pltpu.SemaphoreType.DMA
    flops = 2 * pool_rows * hid * (feats + width) * 2 + 6 * slots * every * width
    loss, query_grad, table_grad = pl.pallas_call(
        functools.partial(step_kernel, n, nb, group),
        out_shape=(
            jax.ShapeDtypeStruct((1, queries), f32),
            jax.ShapeDtypeStruct((queries, width), f32),
            jax.ShapeDtypeStruct((pool_rows, feats), f32),
        ),
        in_specs=[in_vmem, in_any, in_any, in_vmem, in_any, in_vmem, in_vmem, in_vmem],
        out_specs=(in_vmem, in_vmem, in_any),
        scratch_shapes=[
            pltpu.VMEM((pool_rows, feats), bf16),
            pltpu.VMEM((chunks, feats, chunk), bf16),
            pltpu.VMEM((chunks, chunk, width), bf16),
            pltpu.VMEM((chunks, pool_rows, chunk), bf16),
            pltpu.VMEM((pool_rows, width), f32),
            pltpu.VMEM((pool_rows, width), bf16),
            pltpu.VMEM((n, 1, 128), jnp.int32),
            pltpu.VMEM((n, 1, 128), jnp.int32),
            pltpu.VMEM((n, 128), jnp.int32),
            pltpu.VMEM((slots, 1), f32),
            pltpu.VMEM((1, slots), f32),
            pltpu.VMEM((slots, width), bf16),
            pltpu.VMEM((slots, width), bf16),
            pltpu.VMEM((every, width), bf16),
            pltpu.VMEM((slots, 1), f32),
            pltpu.VMEM((slots, every), f32),
            pltpu.VMEM((slots, every), bf16),
            pltpu.VMEM((nb, 1, every), f32),
            pltpu.VMEM((1, every), f32),
            pltpu.VMEM((slots, width), bf16),
            pltpu.VMEM((slots, width), bf16),
            pltpu.VMEM((nb, queries, width), bf16),
            pltpu.VMEM((nb, queries, width), bf16),
            pltpu.VMEM((pool_rows, width), f32),
            pltpu.VMEM((chunks, pool_rows, chunk), bf16),
            pltpu.VMEM((outs, pool_rows, out_cols), f32),
            dma((2 * chunks + 1,)),
            dma((outs,)),
            dma((n,)), dma((n,)), dma((n,)), dma((n,)), dma((n,)), dma((n,)),
            dma((nb,)), dma((nb,)), dma((nb,)), dma((nb,)), dma((nb,)), dma((nb,)),
        ],
        compiler_params=pltpu.CompilerParams(
            collective_id=0, has_side_effects=True, vmem_limit_bytes=56 * 1024 * 1024
        ),
        cost_estimate=pl.CostEstimate(
            flops=flops, bytes_accessed=20_000_000, transcendentals=3_000_000
        ),
        name="retrieval_step",
    )(
        query_emb, item_table, w_in, bias_in.reshape(1, hid), w_out, fetch_rows, fetch_counts,
        pos_slot.reshape(1, queries),
    )
    return (loss.reshape(queries), query_grad, table_grad)


def solution(mesh):
    placed = (
        P(("pool", "blk"), None),
        P(("pool", "blk"), None),
        P(),
        P(),
        P(),
        P(("pool", "blk"), None),
        P(("pool", "blk"), None),
        P(("pool", "blk")),
    )
    return jax.shard_map(
        on_device,
        mesh=mesh,
        in_specs=placed,
        out_specs=(P(("pool", "blk")), P(("pool", "blk"), None), P(("pool", "blk"), None)),
        check_vma=False,
    )
```

```python
import functools

import jax
import jax.numpy as jnp
from jax import lax
from jax.experimental import pallas as pl
from jax.experimental.pallas import tpu as pltpu
from jax.sharding import PartitionSpec as P

logit_scale = 80.0
norm_eps = 1e-06
shift = 4.0
log2e = 1.4426950408889634
ln2 = 0.6931471805599453

MESH = pl.DeviceIdType.MESH
f32 = jnp.float32
bf16 = jnp.bfloat16
NN = (((1,), (0,)), ((), ()))
NT = (((1,), (1,)), ((), ()))
TN = (((0,), (0,)), ((), ()))


def mm(a, b, dims=NN):
    return lax.dot_general(a, b, dims, preferred_element_type=f32)


def iota(shape, dim):
    return lax.broadcasted_iota(jnp.int32, shape, dim)


def step_kernel(
    n, nb, group,
    query_hbm, table_hbm, win_hbm, bias_hbm, wout_hbm, rows_hbm, counts_hbm, pos_hbm,
    loss_out, qgrad_out, tgrad_out,
    query_ref, bias_ref, rows_ref, counts_ref, pos_ref, loss_ref, qgrad_ref, table, win, wout, dsilu, tower, item_vec, idx_send, idx_mid, idx_recv, idx_flat, idx_col, idx_row,
    serve, arrive, group_vec, live_col, expo, coef, sums, lossbuf, inv_buf, picked, grad, ret, vg_send, vg_recv,
    row_grad, pre_grad, out_buf,
    a_sem, w_sem, o_sem, isend, irecv, fsend, frecv, bsend, brecv, qsend, qrecv, ssend, srecv, vsend, vrecv,
):
    p = lax.axis_index("pool")
    b = lax.axis_index("blk")
    cap = rows_ref.shape[0]
    slots = n * cap
    span = group * cap
    groups = n // group
    queries, width = query_ref.shape
    chunks, feats, chunk = win.shape
    pool_rows = table.shape[0]
    outs, out_cols = out_buf.shape[0], out_buf.shape[2]

    def load_table():
        return pltpu.make_async_copy(table_hbm, table, w_sem.at[2 * chunks])

    def load_win(c):
        return pltpu.make_async_copy(
            win_hbm.at[:, pl.ds(pl.multiple_of(c * chunk, chunk), chunk)], win.at[c], w_sem.at[c]
        )

    def load_wout(c):
        return pltpu.make_async_copy(
            wout_hbm.at[pl.ds(pl.multiple_of(c * chunk, chunk), chunk), :],
            wout.at[c],
            w_sem.at[chunks + c],
        )

    def ahead(k):
        return lax.rem(p + k, n)

    def behind(k):
        return lax.rem(p + n - k, n)

    plane = idx_send.shape[1]
    planes = n // plane
    my_plane = p // plane
    my_place = lax.rem(p, plane)

    def hop1_copy(k):
        other = lax.rem(my_plane + k, planes)
        return pltpu.make_async_remote_copy(
            src_ref=idx_send.at[other], dst_ref=idx_mid.at[my_plane], send_sem=isend.at[k],
            recv_sem=irecv.at[k], device_id={"pool": other * plane + my_place},
            device_id_type=MESH,
        )

    def hop1_arrival(k):
        src = lax.rem(my_plane + planes - k, planes)
        return pltpu.make_async_remote_copy(
            src_ref=idx_send.at[src], dst_ref=idx_mid.at[src], send_sem=isend.at[k],
            recv_sem=irecv.at[k], device_id={"pool": src * plane + my_place},
            device_id_type=MESH,
        )

    def hop2_copy(k):
        other = lax.rem(my_place + k, plane)
        return pltpu.make_async_remote_copy(
            src_ref=idx_mid.at[:, other], dst_ref=idx_recv.at[my_place],
            send_sem=isend.at[planes + k], recv_sem=irecv.at[planes + k],
            device_id={"pool": my_plane * plane + other}, device_id_type=MESH,
        )

    def hop2_arrival(k):
        src = lax.rem(my_place + plane - k, plane)
        return pltpu.make_async_remote_copy(
            src_ref=idx_mid.at[:, src], dst_ref=idx_recv.at[src],
            send_sem=isend.at[planes + k], recv_sem=irecv.at[planes + k],
            device_id={"pool": my_plane * plane + src}, device_id_type=MESH,
        )

    def rows_of(k):
        return pl.ds(pl.multiple_of(k * cap, cap), cap)

    def fwd_copy(k):
        return pltpu.make_async_remote_copy(
            src_ref=serve.at[rows_of(k)], dst_ref=arrive.at[rows_of(k)], send_sem=fsend.at[k],
            recv_sem=frecv.at[k], device_id={"pool": behind(k)}, device_id_type=MESH,
        )

    def bwd_copy(k):
        return pltpu.make_async_remote_copy(
            src_ref=grad.at[rows_of(k)], dst_ref=ret.at[rows_of(k)], send_sem=bsend.at[k],
            recv_sem=brecv.at[k], device_id={"pool": ahead(k)}, device_id_type=MESH,
        )

    def block_of(c):
        return pl.ds(pl.multiple_of(c * queries, queries), queries)

    def query_copy(j):
        return pltpu.make_async_remote_copy(
            src_ref=group_vec.at[block_of(b)], dst_ref=group_vec.at[block_of(b)],
            send_sem=qsend.at[j], recv_sem=qrecv.at[j],
            device_id={"blk": lax.rem(b + j, nb)}, device_id_type=MESH,
        )

    def query_arrival(j):
        src = lax.rem(b + nb - j, nb)
        return pltpu.make_async_remote_copy(
            src_ref=group_vec.at[block_of(src)], dst_ref=group_vec.at[block_of(src)],
            send_sem=qsend.at[j], recv_sem=qrecv.at[j],
            device_id={"blk": lax.rem(b + j, nb)}, device_id_type=MESH,
        )

    def sums_copy(j):
        return pltpu.make_async_remote_copy(
            src_ref=sums.at[b], dst_ref=sums.at[b], send_sem=ssend.at[j], recv_sem=srecv.at[j],
            device_id={"blk": lax.rem(b + j, nb)}, device_id_type=MESH,
        )

    def sums_arrival(j):
        src = lax.rem(b + nb - j, nb)
        return pltpu.make_async_remote_copy(
            src_ref=sums.at[src], dst_ref=sums.at[src], send_sem=ssend.at[j],
            recv_sem=srecv.at[j],
            device_id={"blk": lax.rem(b + j, nb)}, device_id_type=MESH,
        )

    def vg_copy(j):
        return pltpu.make_async_remote_copy(
            src_ref=vg_send.at[j], dst_ref=vg_recv.at[j], send_sem=vsend.at[j],
            recv_sem=vrecv.at[j],
            device_id={"blk": lax.rem(b + j, nb)}, device_id_type=MESH,
        )

    def loop(low, high, body):
        lax.fori_loop(low, high, lambda k, _: (body(k), 0)[1], 0)

    small = [
        pltpu.make_async_copy(src, dst, a_sem.at[i])
        for i, (src, dst) in enumerate((
            (rows_hbm, rows_ref), (query_hbm, query_ref), (bias_hbm, bias_ref),
            (counts_hbm, counts_ref), (pos_hbm, pos_ref),
        ))
    ]
    for copy in small:
        copy.start()
    load_table().start()
    loop(0, chunks, lambda c: (load_win(c).start(), load_wout(c).start()))
    barrier = pltpu.get_barrier_semaphore()

    def greet(k):
        pl.semaphore_signal(barrier, inc=1, device_id={"pool": ahead(k)}, device_id_type=MESH)

    def greet_blk(j):
        pl.semaphore_signal(
            barrier, inc=1, device_id={"blk": lax.rem(b + j, nb)}, device_id_type=MESH
        )

    loop(1, n, greet)
    loop(1, nb, greet_blk)

    def parts_of(rows):
        low = lax.rem(rows, 16)
        return (rows - low).astype(f32).astype(bf16), low.astype(f32).astype(bf16)

    small[0].wait()
    turn = (iota((n, n), 0) == iota((n, n), 1)).astype(f32).astype(bf16)
    high, low = parts_of(rows_ref[...])
    idx_flat[...] = jnp.zeros_like(idx_flat)
    idx_flat[:, 0:cap] = (mm(turn, high, NT) + mm(turn, low, NT)).astype(jnp.int32)

    def put_rows(k):
        idx_send[k // plane, lax.rem(k, plane)] = idx_flat[pl.ds(k, 1), :]

    loop(0, n, put_rows)

    def tower_chunk(c):
        load_win(c).wait()
        load_wout(c).wait()
        cols = pl.ds(pl.multiple_of(c * chunk, chunk), chunk)
        pre = mm(table[...], win[c]) + bias_ref[:, cols]
        sig = 1.0 / (1.0 + jnp.exp(-pre))
        act = pre * sig
        dsilu[c] = (sig * (1.0 + pre - act)).astype(bf16)
        tower[...] += mm(act.astype(bf16), wout[c])

    small[1].wait()
    query_f = query_ref[...].astype(f32)
    query_inv = lax.rsqrt(jnp.sum(query_f * query_f, axis=1, keepdims=True) + norm_eps)
    group_vec[block_of(b), :] = (query_f * query_inv).astype(bf16)

    tower[...] = jnp.zeros_like(tower)
    small[2].wait()
    load_table().wait()
    early, middle = max(1, chunks // 3), max(1, chunks // 2)
    loop(0, early, tower_chunk)

    pl.semaphore_wait(barrier, n + nb - 2)
    loop(1, planes, lambda k: hop1_copy(k).start())
    loop(1, nb, lambda j: query_copy(j).start())
    idx_mid[my_plane] = idx_send[my_plane]
    loop(early, middle, tower_chunk)
    loop(1, planes, lambda k: hop1_arrival(k).wait_recv())
    loop(1, plane, lambda k: hop2_copy(k).start())

    def own_place(z):
        idx_recv[my_place, z] = idx_mid[z, my_place]

    loop(0, planes, own_place)
    loop(middle, chunks, tower_chunk)

    tower_out = tower[...]
    item_inv = lax.rsqrt(jnp.sum(tower_out * tower_out, axis=1, keepdims=True) + norm_eps)
    item_vec[...] = (tower_out * item_inv).astype(bf16)

    loop(1, plane, lambda k: hop2_arrival(k).wait_recv())

    def flat(k):
        src = behind(k)
        idx_flat[pl.ds(k, 1), :] = idx_recv[lax.rem(src, plane), src // plane]

    loop(0, n, flat)
    high, low = parts_of(idx_flat[...])
    lanes = idx_flat.shape[1]
    spread = (iota((slots, n), 0) // cap == iota((slots, n), 1)).astype(f32).astype(bf16)
    wide = mm(spread, high) + mm(spread, low)
    idx_col[...] = jnp.sum(
        jnp.where(iota((slots, lanes), 1) == lax.rem(iota((slots, lanes), 0), cap), wide, 0.0),
        axis=1, keepdims=True,
    )
    spread_t = (iota((n, slots), 1) // cap == iota((n, slots), 0)).astype(f32).astype(bf16)
    tall = mm(high, spread_t, TN) + mm(low, spread_t, TN)
    idx_row[...] = jnp.sum(
        jnp.where(iota((lanes, slots), 0) == lax.rem(iota((lanes, slots), 1), cap), tall, 0.0),
        axis=0, keepdims=True,
    )

    def span_of(g):
        return pl.ds(pl.multiple_of(g * span, span), span)

    def serve_group(g):
        pick = (
            idx_col[span_of(g), :] == iota((span, pool_rows), 1).astype(f32)
        ).astype(f32).astype(bf16)
        serve[span_of(g), :] = mm(pick, item_vec[...]).astype(bf16)

        def send(i):
            k = g * group + i

            @pl.when(k > 0)
            def _():
                fwd_copy(k).start()

        loop(0, group, send)

    loop(0, groups, serve_group)
    arrive[rows_of(0), :] = serve[rows_of(0), :]

    small[3].wait()
    small[4].wait()
    counts = counts_ref[...].astype(f32)
    slot_owner = lax.rem(iota((slots, n), 0) // cap + p, n)
    slot_count = jnp.sum(
        jnp.where(slot_owner == iota((slots, n), 1), counts, 0.0), axis=1, keepdims=True
    )
    live_col[...] = (
        lax.rem(iota((slots, 1), 0), cap).astype(f32) < slot_count
    ).astype(f32)
    own_order = iota((n, n), 0)
    other = iota((n, n), 1)
    ends = jnp.sum(jnp.where(other <= own_order, counts, 0.0), axis=1, keepdims=True)
    count_col = jnp.sum(jnp.where(other == own_order, counts, 0.0), axis=1, keepdims=True)
    pos = pos_ref[...].astype(f32)
    past = ends <= pos
    owner = jnp.sum(jnp.where(past, 1.0, 0.0), axis=0, keepdims=True)
    start = jnp.sum(jnp.where(past, count_col, 0.0), axis=0, keepdims=True)
    owner_rel = lax.rem(owner.astype(jnp.int32) + (n - p), n)
    target = owner_rel * cap + (pos - start).astype(jnp.int32)

    loop(1, nb, lambda j: query_arrival(j).wait_recv())
    all_queries = nb * queries
    sums[b] = jnp.zeros((1, all_queries), f32)
    picked[...] = jnp.zeros_like(picked)

    def hits(g):
        return iota((span, queries), 0) + g * span == target

    def score_group(g):
        def arrival(i):
            k = g * group + i

            @pl.when(k > 0)
            def _():
                fwd_copy(k).wait_recv()

        loop(0, group, arrival)
        vecs = arrive[span_of(g), :]
        scores = mm(vecs, group_vec[...], NT)
        part = jnp.exp2(scores * (logit_scale * log2e) - shift) * live_col[span_of(g), :]
        expo[span_of(g), :] = part
        sums[b] = sums[b] + jnp.sum(part, axis=0, keepdims=True)
        own = mm(vecs, group_vec[block_of(b), :], NT)
        picked[...] += jnp.sum(jnp.where(hits(g), own, 0.0), axis=0, keepdims=True)

    loop(0, groups, score_group)
    loop(1, nb, lambda j: sums_copy(j).start())
    loop(1, nb, lambda j: sums_arrival(j).wait_recv())
    total = sums[0]
    for j in range(1, nb):
        total = total + sums[j]
    inv_total = 1.0 / total
    inv_buf[...] = inv_total
    lossbuf[...] = jnp.log(total) + shift * ln2
    loss_ref[...] = lossbuf[:, block_of(b)] - logit_scale * picked[...]
    loss_copy = pltpu.make_async_copy(loss_ref, loss_out, o_sem.at[outs])
    loss_copy.start()

    def coef_group(g):
        coef[span_of(g), :] = (expo[span_of(g), :] * inv_total).astype(bf16)
        coef[span_of(g), block_of(b)] = (
            expo[span_of(g), block_of(b)] * inv_buf[:, block_of(b)] - jnp.where(hits(g), 1.0, 0.0)
        ).astype(bf16)
        grad[span_of(g), :] = (logit_scale * mm(coef[span_of(g), :], group_vec[...])).astype(bf16)

        def send(i):
            k = g * group + i

            @pl.when(k > 0)
            def _():
                bwd_copy(k).start()

        loop(0, group, send)

    loop(0, groups, coef_group)
    ret[rows_of(0), :] = grad[rows_of(0), :]

    def part_of(c):
        return logit_scale * mm(coef[:, block_of(c)], arrive[...], TN)

    def send_part(j):
        vg_send[j] = part_of(lax.rem(b + j, nb)).astype(bf16)
        vg_copy(j).start()

    loop(1, nb, send_part)
    vec_grad = part_of(b)

    row_grad[...] = jnp.zeros_like(row_grad)

    def sum_group(g):
        def arrival(i):
            k = g * group + i

            @pl.when(k > 0)
            def _():
                bwd_copy(k).wait_recv()

        loop(0, group, arrival)
        pick_t = (
            iota((pool_rows, span), 0).astype(f32) == idx_row[:, span_of(g)]
        ).astype(f32).astype(bf16)
        row_grad[...] += mm(pick_t, ret[span_of(g), :])

    loop(0, groups // 2, sum_group)
    loop(1, nb, lambda j: vg_copy(j).wait_recv())
    for j in range(1, nb):
        vec_grad = vec_grad + vg_recv[j].astype(f32)
    query_f = query_ref[...].astype(f32)
    qgrad_ref[...] = vec_grad * query_inv - query_f * (query_inv * query_inv * query_inv) * jnp.sum(
        query_f * vec_grad, axis=1, keepdims=True
    )
    qgrad_copy = pltpu.make_async_copy(qgrad_ref, qgrad_out, o_sem.at[outs + 1])
    qgrad_copy.start()
    loop(groups // 2, groups, sum_group)

    tower_out = tower[...]
    item_inv = lax.rsqrt(jnp.sum(tower_out * tower_out, axis=1, keepdims=True) + norm_eps)
    summed = row_grad[...]
    item_vec[...] = (
        summed * item_inv
        - tower_out * (item_inv * item_inv * item_inv)
        * jnp.sum(tower_out * summed, axis=1, keepdims=True)
    ).astype(bf16)

    def back_chunk(c):
        pre_grad[c] = (mm(item_vec[...], wout[c], NT) * dsilu[c].astype(f32)).astype(bf16)

    loop(0, chunks, back_chunk)

    def out_copy(f):
        return pltpu.make_async_copy(
            out_buf.at[f],
            tgrad_out.at[:, pl.ds(pl.multiple_of(f * out_cols, out_cols), out_cols)],
            o_sem.at[f],
        )

    def out_block(f):
        rows = pl.ds(pl.multiple_of(f * out_cols, out_cols), out_cols)
        total = mm(pre_grad[0], win[0, rows, :], NT)
        for c in range(1, chunks):
            total = total + mm(pre_grad[c], win[c, rows, :], NT)
        out_buf[f] = total
        out_copy(f).start()

    loop(0, outs, out_block)

    loop(1, planes, lambda k: hop1_copy(k).wait_send())
    loop(1, plane, lambda k: hop2_copy(k).wait_send())
    loop(1, n, lambda k: (fwd_copy(k).wait_send(), bwd_copy(k).wait_send()))
    loop(
        1, nb,
        lambda j: (query_copy(j).wait_send(), sums_copy(j).wait_send(), vg_copy(j).wait_send()),
    )
    loss_copy.wait()
    qgrad_copy.wait()
    loop(0, outs, lambda f: out_copy(f).wait())


def copy_kernel(
    loss_in, qgrad_in, tgrad_in, loss_out, qgrad_out, tgrad_out, loss_ref, qgrad_ref, tgrad_ref,
    in_sem, out_sem
):
    parts = out_sem.shape[0] - 2
    rows = tgrad_ref.shape[0] // parts
    moves = [
        (tgrad_in.at[pl.ds(i * rows, rows)], tgrad_ref.at[pl.ds(i * rows, rows)],
         tgrad_out.at[pl.ds(i * rows, rows)])
        for i in range(parts)
    ]
    moves += [(qgrad_in, qgrad_ref, qgrad_out), (loss_in, loss_ref, loss_out)]
    loads = [
        pltpu.make_async_copy(src, mid, in_sem.at[i]) for i, (src, mid, _) in enumerate(moves)
    ]
    saves = [
        pltpu.make_async_copy(mid, dst, out_sem.at[i]) for i, (_, mid, dst) in enumerate(moves)
    ]
    for load in loads:
        load.start()
    for load, save in zip(loads, saves):
        load.wait()
        save.start()
    for save in saves:
        save.wait()


def on_device(query_emb, item_table, w_in, bias_in, w_out, fetch_rows, fetch_counts, pos_slot):
    n = lax.axis_size("pool")
    nb = lax.axis_size("blk")
    cap = fetch_rows.shape[1]
    slots = n * cap
    queries, width = query_emb.shape
    pool_rows, feats = item_table.shape
    hid = w_in.shape[1]
    chunk = min(512, hid)
    chunks = hid // chunk
    group = min(16, n // 2)
    plane = 8 if n % 8 == 0 and n > 8 else 2
    out_cols = min(256, feats)
    outs = feats // out_cols
    every = nb * queries
    in_hbm = pl.BlockSpec(memory_space=pltpu.HBM)
    dma = pltpu.SemaphoreType.DMA
    flops = 2 * pool_rows * hid * (feats + width) * 2 + 6 * slots * every * width
    loss, query_grad, table_grad = pl.pallas_call(
        functools.partial(step_kernel, n, nb, group),
        out_shape=(
            jax.ShapeDtypeStruct((1, queries), f32),
            jax.ShapeDtypeStruct((queries, width), f32),
            jax.ShapeDtypeStruct((pool_rows, feats), f32),
        ),
        in_specs=[in_hbm] * 8,
        out_specs=(in_hbm, in_hbm, in_hbm),
        scratch_shapes=[
            pltpu.VMEM((queries, width), bf16),
            pltpu.VMEM((1, hid), f32),
            pltpu.VMEM((cap, n), jnp.int32),
            pltpu.VMEM((1, n), jnp.int32),
            pltpu.VMEM((1, queries), jnp.int32),
            pltpu.VMEM((1, queries), f32),
            pltpu.VMEM((queries, width), f32),
            pltpu.VMEM((pool_rows, feats), bf16),
            pltpu.VMEM((chunks, feats, chunk), bf16),
            pltpu.VMEM((chunks, chunk, width), bf16),
            pltpu.VMEM((chunks, pool_rows, chunk), bf16),
            pltpu.VMEM((pool_rows, width), f32),
            pltpu.VMEM((pool_rows, width), bf16),
            pltpu.VMEM((n // plane, plane, 1, 128), jnp.int32),
            pltpu.VMEM((n // plane, plane, 1, 128), jnp.int32),
            pltpu.VMEM((plane, n // plane, 1, 128), jnp.int32),
            pltpu.VMEM((n, 128), jnp.int32),
            pltpu.VMEM((slots, 1), f32),
            pltpu.VMEM((1, slots), f32),
            pltpu.VMEM((slots, width), bf16),
            pltpu.VMEM((slots, width), bf16),
            pltpu.VMEM((every, width), bf16),
            pltpu.VMEM((slots, 1), f32),
            pltpu.VMEM((slots, every), f32),
            pltpu.VMEM((slots, every), bf16),
            pltpu.VMEM((nb, 1, every), f32),
            pltpu.VMEM((1, every), f32),
            pltpu.VMEM((1, every), f32),
            pltpu.VMEM((1, queries), f32),
            pltpu.VMEM((slots, width), bf16),
            pltpu.VMEM((slots, width), bf16),
            pltpu.VMEM((nb, queries, width), bf16),
            pltpu.VMEM((nb, queries, width), bf16),
            pltpu.VMEM((pool_rows, width), f32),
            pltpu.VMEM((chunks, pool_rows, chunk), bf16),
            pltpu.VMEM((outs, pool_rows, out_cols), f32),
            dma((5,)),
            dma((2 * chunks + 1,)),
            dma((outs + 2,)),
            dma((plane + n // plane,)), dma((plane + n // plane,)),
            dma((n,)), dma((n,)), dma((n,)), dma((n,)),
            dma((nb,)), dma((nb,)), dma((nb,)), dma((nb,)), dma((nb,)), dma((nb,)),
        ],
        compiler_params=pltpu.CompilerParams(
            collective_id=0, has_side_effects=True, vmem_limit_bytes=60 * 1024 * 1024
        ),
        cost_estimate=pl.CostEstimate(
            flops=flops, bytes_accessed=20_000_000, transcendentals=3_000_000
        ),
        name="retrieval_step",
    )(
        query_emb, item_table, w_in, bias_in.reshape(1, hid), w_out, fetch_rows.T, fetch_counts,
        pos_slot.reshape(1, queries),
    )
    parts = 4
    loss, query_grad, table_grad = pl.pallas_call(
        copy_kernel,
        out_shape=(
            jax.ShapeDtypeStruct((1, queries), f32),
            jax.ShapeDtypeStruct((queries, width), f32),
            jax.ShapeDtypeStruct((pool_rows, feats), f32),
        ),
        in_specs=[in_hbm] * 3,
        out_specs=(in_hbm, in_hbm, in_hbm),
        scratch_shapes=[
            pltpu.VMEM((1, queries), f32),
            pltpu.VMEM((queries, width), f32),
            pltpu.VMEM((pool_rows, feats), f32),
            dma((parts + 2,)),
            dma((parts + 2,)),
        ],
        compiler_params=pltpu.CompilerParams(vmem_limit_bytes=60 * 1024 * 1024),
        cost_estimate=pl.CostEstimate(flops=0, bytes_accessed=6_000_000, transcendentals=0),
        name="results",
    )(loss, query_grad, table_grad)
    return (loss.reshape(queries), query_grad, table_grad)


def solution(mesh):
    placed = (
        P(("pool", "blk"), None),
        P(("pool", "blk"), None),
        P(),
        P(),
        P(),
        P(("pool", "blk"), None),
        P(("pool", "blk"), None),
        P(("pool", "blk")),
    )
    return jax.shard_map(
        on_device,
        mesh=mesh,
        in_specs=placed,
        out_specs=(P(("pool", "blk")), P(("pool", "blk"), None), P(("pool", "blk"), None)),
        check_vma=False,
    )
```

```python
import functools

import jax
import jax.numpy as jnp
from jax import lax
from jax.experimental import pallas as pl
from jax.experimental.pallas import tpu as pltpu
from jax.sharding import PartitionSpec as P

logit_scale = 80.0
norm_eps = 1e-06
shift = 4.0
log2e = 1.4426950408889634
ln2 = 0.6931471805599453

MESH = pl.DeviceIdType.MESH
f32 = jnp.float32
bf16 = jnp.bfloat16
NN = (((1,), (0,)), ((), ()))
NT = (((1,), (1,)), ((), ()))
TN = (((0,), (0,)), ((), ()))


def mm(a, b, dims=NN):
    return lax.dot_general(a, b, dims, preferred_element_type=f32)


def iota(shape, dim):
    return lax.broadcasted_iota(jnp.int32, shape, dim)


def step_kernel(
    n, nb, group,
    query_hbm, table_hbm, win_hbm, bias_hbm, wout_hbm, rows_hbm, counts_hbm, pos_hbm,
    loss_out, qgrad_out, tgrad_out,
    query_ref, bias_ref, rows_ref, counts_ref, pos_ref, loss_ref, qgrad_ref, table, win, wout, dsilu, tower, item_vec, idx_send, idx_mid, idx_recv, idx_flat, idx_col, idx_row,
    serve, arrive, group_vec, live_col, expo, coef, sums, lossbuf, inv_buf, picked, grad, ret, vg_send, vg_recv,
    row_grad, pre_grad, out_buf,
    a_sem, w_sem, o_sem, isend, irecv, fsend, frecv, bsend, brecv, qsend, qrecv, ssend, srecv, vsend, vrecv,
):
    p = lax.axis_index("pool")
    b = lax.axis_index("blk")
    cap = rows_ref.shape[0]
    slots = n * cap
    span = group * cap
    groups = n // group
    queries, width = query_ref.shape
    chunks, feats, chunk = win.shape
    pool_rows = table.shape[0]
    outs, out_cols = out_buf.shape[0], out_buf.shape[2]

    def load_table():
        return pltpu.make_async_copy(table_hbm, table, w_sem.at[2 * chunks])

    def load_win(c):
        return pltpu.make_async_copy(
            win_hbm.at[:, pl.ds(pl.multiple_of(c * chunk, chunk), chunk)], win.at[c], w_sem.at[c]
        )

    def load_wout(c):
        return pltpu.make_async_copy(
            wout_hbm.at[pl.ds(pl.multiple_of(c * chunk, chunk), chunk), :],
            wout.at[c],
            w_sem.at[chunks + c],
        )

    def ahead(k):
        return lax.rem(p + k, n)

    def behind(k):
        return lax.rem(p + n - k, n)

    planes, plane = idx_recv.shape[0], idx_recv.shape[1]
    my_plane = p // plane
    my_place = lax.rem(p, plane)

    def place_at(k):
        return lax.rem(my_place + k, plane)

    def plane_at(k):
        return lax.rem(my_plane + k, planes)

    def hop1_copy(k):
        other = place_at(k)
        return pltpu.make_async_remote_copy(
            src_ref=idx_send.at[other], dst_ref=idx_mid.at[my_place], send_sem=isend.at[k],
            recv_sem=irecv.at[k], device_id={"pool": my_plane * plane + other},
            device_id_type=MESH,
        )

    def hop1_arrival(k):
        src = place_at(plane - k)
        return pltpu.make_async_remote_copy(
            src_ref=idx_send.at[src], dst_ref=idx_mid.at[src], send_sem=isend.at[k],
            recv_sem=irecv.at[k], device_id={"pool": my_plane * plane + src},
            device_id_type=MESH,
        )

    def hop2_copy(k):
        other = plane_at(k)
        return pltpu.make_async_remote_copy(
            src_ref=idx_mid.at[:, other], dst_ref=idx_recv.at[my_plane],
            send_sem=isend.at[plane + k], recv_sem=irecv.at[plane + k],
            device_id={"pool": other * plane + my_place}, device_id_type=MESH,
        )

    def hop2_arrival(k):
        src = plane_at(planes - k)
        return pltpu.make_async_remote_copy(
            src_ref=idx_mid.at[:, src], dst_ref=idx_recv.at[src],
            send_sem=isend.at[plane + k], recv_sem=irecv.at[plane + k],
            device_id={"pool": src * plane + my_place}, device_id_type=MESH,
        )

    def rows_of(k):
        return pl.ds(pl.multiple_of(k * cap, cap), cap)

    def fwd_copy(k):
        return pltpu.make_async_remote_copy(
            src_ref=serve.at[rows_of(k)], dst_ref=arrive.at[rows_of(k)], send_sem=fsend.at[k],
            recv_sem=frecv.at[k], device_id={"pool": behind(k)}, device_id_type=MESH,
        )

    def bwd_copy(k):
        return pltpu.make_async_remote_copy(
            src_ref=grad.at[rows_of(k)], dst_ref=ret.at[rows_of(k)], send_sem=bsend.at[k],
            recv_sem=brecv.at[k], device_id={"pool": ahead(k)}, device_id_type=MESH,
        )

    def block_of(c):
        return pl.ds(pl.multiple_of(c * queries, queries), queries)

    def query_copy(j):
        return pltpu.make_async_remote_copy(
            src_ref=group_vec.at[block_of(b)], dst_ref=group_vec.at[block_of(b)],
            send_sem=qsend.at[j], recv_sem=qrecv.at[j],
            device_id={"blk": lax.rem(b + j, nb)}, device_id_type=MESH,
        )

    def query_arrival(j):
        src = lax.rem(b + nb - j, nb)
        return pltpu.make_async_remote_copy(
            src_ref=group_vec.at[block_of(src)], dst_ref=group_vec.at[block_of(src)],
            send_sem=qsend.at[j], recv_sem=qrecv.at[j],
            device_id={"blk": lax.rem(b + j, nb)}, device_id_type=MESH,
        )

    def sums_copy(j):
        return pltpu.make_async_remote_copy(
            src_ref=sums.at[b], dst_ref=sums.at[b], send_sem=ssend.at[j], recv_sem=srecv.at[j],
            device_id={"blk": lax.rem(b + j, nb)}, device_id_type=MESH,
        )

    def sums_arrival(j):
        src = lax.rem(b + nb - j, nb)
        return pltpu.make_async_remote_copy(
            src_ref=sums.at[src], dst_ref=sums.at[src], send_sem=ssend.at[j],
            recv_sem=srecv.at[j],
            device_id={"blk": lax.rem(b + j, nb)}, device_id_type=MESH,
        )

    def vg_copy(j):
        return pltpu.make_async_remote_copy(
            src_ref=vg_send.at[j], dst_ref=vg_recv.at[j], send_sem=vsend.at[j],
            recv_sem=vrecv.at[j],
            device_id={"blk": lax.rem(b + j, nb)}, device_id_type=MESH,
        )

    def loop(low, high, body):
        lax.fori_loop(low, high, lambda k, _: (body(k), 0)[1], 0)

    barrier = pltpu.get_barrier_semaphore()

    def greet(device):
        pl.semaphore_signal(barrier, inc=1, device_id=device, device_id_type=MESH)

    loop(1, plane, lambda k: greet({"pool": my_plane * plane + place_at(k)}))
    loop(1, planes, lambda k: greet({"pool": plane_at(k) * plane + my_place}))
    loop(1, nb, lambda j: greet({"blk": lax.rem(b + j, nb)}))

    small = [
        pltpu.make_async_copy(src, dst, a_sem.at[i])
        for i, (src, dst) in enumerate((
            (rows_hbm, rows_ref), (query_hbm, query_ref), (bias_hbm, bias_ref),
            (counts_hbm, counts_ref), (pos_hbm, pos_ref),
        ))
    ]
    for copy in small:
        copy.start()
    load_table().start()
    loop(0, chunks, lambda c: (load_win(c).start(), load_wout(c).start()))

    def parts_of(rows):
        low = lax.rem(rows, 16)
        return (rows - low).astype(f32).astype(bf16), low.astype(f32).astype(bf16)

    small[0].wait()
    turn = (iota((n, n), 0) == iota((n, n), 1)).astype(f32).astype(bf16)
    high, low = parts_of(rows_ref[...])
    idx_flat[...] = jnp.zeros_like(idx_flat)
    idx_flat[:, 0:cap] = (mm(turn, high, NT) + mm(turn, low, NT)).astype(jnp.int32)

    def put_rows(k):
        idx_send[lax.rem(k, plane), k // plane] = idx_flat[pl.ds(k, 1), :]

    loop(0, n, put_rows)

    def tower_chunk(c):
        load_win(c).wait()
        load_wout(c).wait()
        cols = pl.ds(pl.multiple_of(c * chunk, chunk), chunk)
        half = 0.5 * (mm(table[...], win[c]) + bias_ref[:, cols])
        tanh = jnp.tanh(half)
        bent = half * tanh
        tower[...] += mm((half + bent).astype(bf16), wout[c])
        dsilu[c] = ((0.5 + 0.5 * tanh) * (1.0 + (half - bent))).astype(bf16)

    pl.semaphore_wait(barrier, plane + planes + nb - 3)
    loop(1, plane, lambda k: hop1_copy(k).start())
    idx_mid[my_place] = idx_send[my_place]

    small[1].wait()
    query_f = query_ref[...].astype(f32)
    query_inv = lax.rsqrt(jnp.sum(query_f * query_f, axis=1, keepdims=True) + norm_eps)
    group_vec[block_of(b), :] = (query_f * query_inv).astype(bf16)

    tower[...] = jnp.zeros_like(tower)
    small[2].wait()
    load_table().wait()
    loop(0, 1, tower_chunk)
    loop(1, plane, lambda k: hop1_arrival(k).wait_recv())
    loop(1, planes, lambda k: hop2_copy(k).start())

    def own_plane(r):
        idx_recv[my_plane, r] = idx_mid[r, my_plane]

    loop(0, plane, own_plane)
    loop(1, chunks, tower_chunk)

    tower_out = tower[...]
    item_inv = lax.rsqrt(jnp.sum(tower_out * tower_out, axis=1, keepdims=True) + norm_eps)
    item_vec[...] = (tower_out * item_inv).astype(bf16)

    loop(1, planes, lambda k: hop2_arrival(k).wait_recv())

    def flat(k):
        src = behind(k)
        idx_flat[pl.ds(k, 1), :] = idx_recv[src // plane, lax.rem(src, plane)]

    loop(0, n, flat)
    high, low = parts_of(idx_flat[...])
    lanes = idx_flat.shape[1]
    spread = (iota((slots, n), 0) // cap == iota((slots, n), 1)).astype(f32).astype(bf16)
    wide = mm(spread, high) + mm(spread, low)
    idx_col[...] = jnp.sum(
        jnp.where(iota((slots, lanes), 1) == lax.rem(iota((slots, lanes), 0), cap), wide, 0.0),
        axis=1, keepdims=True,
    )
    def span_of(g):
        return pl.ds(pl.multiple_of(g * span, span), span)

    def serve_group(g):
        pick = (
            idx_col[span_of(g), :] == iota((span, pool_rows), 1).astype(f32)
        ).astype(f32).astype(bf16)
        serve[span_of(g), :] = mm(pick, item_vec[...]).astype(bf16)

        def send(i):
            k = g * group + i

            @pl.when(k > 0)
            def _():
                fwd_copy(k).start()

        loop(0, group, send)

        @pl.when(g < nb - 1)
        def _():
            query_copy(g + 1).start()

    loop(0, groups, serve_group)
    arrive[rows_of(0), :] = serve[rows_of(0), :]
    spread_t = (iota((n, slots), 1) // cap == iota((n, slots), 0)).astype(f32).astype(bf16)
    tall = mm(high, spread_t, TN) + mm(low, spread_t, TN)
    idx_row[...] = jnp.sum(
        jnp.where(iota((lanes, slots), 0) == lax.rem(iota((lanes, slots), 1), cap), tall, 0.0),
        axis=0, keepdims=True,
    )


    small[3].wait()
    small[4].wait()
    counts = counts_ref[...].astype(f32)
    slot_owner = lax.rem(iota((slots, n), 0) // cap + p, n)
    slot_count = jnp.sum(
        jnp.where(slot_owner == iota((slots, n), 1), counts, 0.0), axis=1, keepdims=True
    )
    live_col[...] = (
        lax.rem(iota((slots, 1), 0), cap).astype(f32) < slot_count
    ).astype(f32)
    own_order = iota((n, n), 0)
    other = iota((n, n), 1)
    ends = jnp.sum(jnp.where(other <= own_order, counts, 0.0), axis=1, keepdims=True)
    count_col = jnp.sum(jnp.where(other == own_order, counts, 0.0), axis=1, keepdims=True)
    pos = pos_ref[...].astype(f32)
    past = ends <= pos
    owner = jnp.sum(jnp.where(past, 1.0, 0.0), axis=0, keepdims=True)
    start = jnp.sum(jnp.where(past, count_col, 0.0), axis=0, keepdims=True)
    owner_rel = lax.rem(owner.astype(jnp.int32) + (n - p), n)
    target = owner_rel * cap + (pos - start).astype(jnp.int32)

    loop(1, nb, lambda j: query_arrival(j).wait_recv())
    all_queries = nb * queries
    sums[b] = jnp.zeros((1, all_queries), f32)
    picked[...] = jnp.zeros_like(picked)

    def hits(g):
        return iota((span, queries), 0) + g * span == target

    def score_group(g):
        def arrival(i):
            k = g * group + i

            @pl.when(k > 0)
            def _():
                fwd_copy(k).wait_recv()

        loop(0, group, arrival)
        vecs = arrive[span_of(g), :]
        scores = mm(vecs, group_vec[...], NT)
        part = jnp.exp2(scores * (logit_scale * log2e) - shift) * live_col[span_of(g), :]
        expo[span_of(g), :] = part
        sums[b] = sums[b] + jnp.sum(part, axis=0, keepdims=True)
        own = mm(vecs, group_vec[block_of(b), :], NT)
        picked[...] += jnp.sum(jnp.where(hits(g), own, 0.0), axis=0, keepdims=True)

    loop(0, groups, score_group)
    loop(1, nb, lambda j: sums_copy(j).start())
    loop(1, nb, lambda j: sums_arrival(j).wait_recv())
    total = sums[0]
    for j in range(1, nb):
        total = total + sums[j]
    inv_total = 1.0 / total
    inv_buf[...] = inv_total
    lossbuf[...] = jnp.log(total) + shift * ln2
    loss_ref[...] = lossbuf[:, block_of(b)] - logit_scale * picked[...]
    loss_copy = pltpu.make_async_copy(loss_ref, loss_out, o_sem.at[outs])
    loss_copy.start()

    def coef_group(g):
        coef[span_of(g), :] = (expo[span_of(g), :] * inv_total).astype(bf16)
        coef[span_of(g), block_of(b)] = (
            expo[span_of(g), block_of(b)] * inv_buf[:, block_of(b)] - jnp.where(hits(g), 1.0, 0.0)
        ).astype(bf16)
        grad[span_of(g), :] = (logit_scale * mm(coef[span_of(g), :], group_vec[...])).astype(bf16)

        def send(i):
            k = g * group + i

            @pl.when(k > 0)
            def _():
                bwd_copy(k).start()

        loop(0, group, send)

    loop(0, groups, coef_group)
    ret[rows_of(0), :] = grad[rows_of(0), :]

    def part_of(c):
        return logit_scale * mm(coef[:, block_of(c)], arrive[...], TN)

    def send_part(j):
        vg_send[j] = part_of(lax.rem(b + j, nb)).astype(bf16)
        vg_copy(j).start()

    loop(1, nb, send_part)
    vec_grad = part_of(b)

    row_grad[...] = jnp.zeros_like(row_grad)

    def sum_group(g):
        def arrival(i):
            k = g * group + i

            @pl.when(k > 0)
            def _():
                bwd_copy(k).wait_recv()

        loop(0, group, arrival)
        pick_t = (
            iota((pool_rows, span), 0).astype(f32) == idx_row[:, span_of(g)]
        ).astype(f32).astype(bf16)
        row_grad[...] += mm(pick_t, ret[span_of(g), :])

    loop(0, groups // 2, sum_group)
    loop(1, nb, lambda j: vg_copy(j).wait_recv())
    for j in range(1, nb):
        vec_grad = vec_grad + vg_recv[j].astype(f32)
    query_f = query_ref[...].astype(f32)
    qgrad_ref[...] = vec_grad * query_inv - query_f * (query_inv * query_inv * query_inv) * jnp.sum(
        query_f * vec_grad, axis=1, keepdims=True
    )
    qgrad_copy = pltpu.make_async_copy(qgrad_ref, qgrad_out, o_sem.at[outs + 1])
    qgrad_copy.start()
    loop(groups // 2, groups, sum_group)

    tower_out = tower[...]
    item_inv = lax.rsqrt(jnp.sum(tower_out * tower_out, axis=1, keepdims=True) + norm_eps)
    summed = row_grad[...]
    item_vec[...] = (
        summed * item_inv
        - tower_out * (item_inv * item_inv * item_inv)
        * jnp.sum(tower_out * summed, axis=1, keepdims=True)
    ).astype(bf16)

    def back_chunk(c):
        pre_grad[c] = (mm(item_vec[...], wout[c], NT) * dsilu[c].astype(f32)).astype(bf16)

    loop(0, chunks // 2, lambda i: (back_chunk(2 * i), back_chunk(2 * i + 1)))

    def out_copy(f):
        return pltpu.make_async_copy(
            out_buf.at[f],
            tgrad_out.at[:, pl.ds(pl.multiple_of(f * out_cols, out_cols), out_cols)],
            o_sem.at[f],
        )

    def out_block(f):
        rows = pl.ds(pl.multiple_of(f * out_cols, out_cols), out_cols)
        total = mm(pre_grad[0], win[0, rows, :], NT)
        for c in range(1, chunks):
            total = total + mm(pre_grad[c], win[c, rows, :], NT)
        out_buf[f] = total
        out_copy(f).start()

    if outs % 2:
        loop(0, outs, out_block)
    else:
        loop(0, outs // 2, lambda i: (out_block(2 * i), out_block(2 * i + 1)))

    loop(1, plane, lambda k: hop1_copy(k).wait_send())
    loop(1, planes, lambda k: hop2_copy(k).wait_send())
    loop(1, n, lambda k: (fwd_copy(k).wait_send(), bwd_copy(k).wait_send()))
    loop(
        1, nb,
        lambda j: (query_copy(j).wait_send(), sums_copy(j).wait_send(), vg_copy(j).wait_send()),
    )
    loss_copy.wait()
    qgrad_copy.wait()
    loop(0, outs, lambda f: out_copy(f).wait())


def copy_kernel(
    loss_in, qgrad_in, tgrad_in, loss_out, qgrad_out, tgrad_out, loss_ref, qgrad_ref, tgrad_ref,
    in_sem, out_sem
):
    parts = out_sem.shape[0] - 2
    rows = tgrad_ref.shape[0] // parts
    moves = [
        (tgrad_in.at[pl.ds(i * rows, rows)], tgrad_ref.at[pl.ds(i * rows, rows)],
         tgrad_out.at[pl.ds(i * rows, rows)])
        for i in range(parts)
    ]
    moves += [(qgrad_in, qgrad_ref, qgrad_out), (loss_in, loss_ref, loss_out)]
    loads = [
        pltpu.make_async_copy(src, mid, in_sem.at[i]) for i, (src, mid, _) in enumerate(moves)
    ]
    saves = [
        pltpu.make_async_copy(mid, dst, out_sem.at[i]) for i, (_, mid, dst) in enumerate(moves)
    ]
    for load in loads:
        load.start()
    for load, save in zip(loads, saves):
        load.wait()
        save.start()
    for save in saves:
        save.wait()


def on_device(query_emb, item_table, w_in, bias_in, w_out, fetch_rows, fetch_counts, pos_slot):
    n = lax.axis_size("pool")
    nb = lax.axis_size("blk")
    cap = fetch_rows.shape[1]
    slots = n * cap
    queries, width = query_emb.shape
    pool_rows, feats = item_table.shape
    hid = w_in.shape[1]
    chunk = min(512, hid)
    chunks = hid // chunk
    group = min(16, n // 2)
    plane = 8 if n % 8 == 0 and n > 8 else 2
    out_cols = min(256, feats)
    outs = feats // out_cols
    every = nb * queries
    in_hbm = pl.BlockSpec(memory_space=pltpu.HBM)
    dma = pltpu.SemaphoreType.DMA
    flops = 2 * pool_rows * hid * (feats + width) * 2 + 6 * slots * every * width
    loss, query_grad, table_grad = pl.pallas_call(
        functools.partial(step_kernel, n, nb, group),
        out_shape=(
            jax.ShapeDtypeStruct((1, queries), f32),
            jax.ShapeDtypeStruct((queries, width), f32),
            jax.ShapeDtypeStruct((pool_rows, feats), f32),
        ),
        in_specs=[in_hbm] * 8,
        out_specs=(in_hbm, in_hbm, in_hbm),
        scratch_shapes=[
            pltpu.VMEM((queries, width), bf16),
            pltpu.VMEM((1, hid), f32),
            pltpu.VMEM((cap, n), jnp.int32),
            pltpu.VMEM((1, n), jnp.int32),
            pltpu.VMEM((1, queries), jnp.int32),
            pltpu.VMEM((1, queries), f32),
            pltpu.VMEM((queries, width), f32),
            pltpu.VMEM((pool_rows, feats), bf16),
            pltpu.VMEM((chunks, feats, chunk), bf16),
            pltpu.VMEM((chunks, chunk, width), bf16),
            pltpu.VMEM((chunks, pool_rows, chunk), bf16),
            pltpu.VMEM((pool_rows, width), f32),
            pltpu.VMEM((pool_rows, width), bf16),
            pltpu.VMEM((plane, n // plane, 1, 128), jnp.int32),
            pltpu.VMEM((plane, n // plane, 1, 128), jnp.int32),
            pltpu.VMEM((n // plane, plane, 1, 128), jnp.int32),
            pltpu.VMEM((n, 128), jnp.int32),
            pltpu.VMEM((slots, 1), f32),
            pltpu.VMEM((1, slots), f32),
            pltpu.VMEM((slots, width), bf16),
            pltpu.VMEM((slots, width), bf16),
            pltpu.VMEM((every, width), bf16),
            pltpu.VMEM((slots, 1), f32),
            pltpu.VMEM((slots, every), f32),
            pltpu.VMEM((slots, every), bf16),
            pltpu.VMEM((nb, 1, every), f32),
            pltpu.VMEM((1, every), f32),
            pltpu.VMEM((1, every), f32),
            pltpu.VMEM((1, queries), f32),
            pltpu.VMEM((slots, width), bf16),
            pltpu.VMEM((slots, width), bf16),
            pltpu.VMEM((nb, queries, width), bf16),
            pltpu.VMEM((nb, queries, width), bf16),
            pltpu.VMEM((pool_rows, width), f32),
            pltpu.VMEM((chunks, pool_rows, chunk), bf16),
            pltpu.VMEM((outs, pool_rows, out_cols), f32),
            dma((5,)),
            dma((2 * chunks + 1,)),
            dma((outs + 2,)),
            dma((plane + n // plane,)), dma((plane + n // plane,)),
            dma((n,)), dma((n,)), dma((n,)), dma((n,)),
            dma((nb,)), dma((nb,)), dma((nb,)), dma((nb,)), dma((nb,)), dma((nb,)),
        ],
        compiler_params=pltpu.CompilerParams(
            collective_id=0, has_side_effects=True, vmem_limit_bytes=60 * 1024 * 1024
        ),
        cost_estimate=pl.CostEstimate(
            flops=flops, bytes_accessed=20_000_000, transcendentals=3_000_000
        ),
        name="retrieval_step",
    )(
        query_emb, item_table, w_in, bias_in.reshape(1, hid), w_out, fetch_rows.T, fetch_counts,
        pos_slot.reshape(1, queries),
    )
    parts = 4
    loss, query_grad, table_grad = pl.pallas_call(
        copy_kernel,
        out_shape=(
            jax.ShapeDtypeStruct((1, queries), f32),
            jax.ShapeDtypeStruct((queries, width), f32),
            jax.ShapeDtypeStruct((pool_rows, feats), f32),
        ),
        in_specs=[in_hbm] * 3,
        out_specs=(in_hbm, in_hbm, in_hbm),
        scratch_shapes=[
            pltpu.VMEM((1, queries), f32),
            pltpu.VMEM((queries, width), f32),
            pltpu.VMEM((pool_rows, feats), f32),
            dma((parts + 2,)),
            dma((parts + 2,)),
        ],
        compiler_params=pltpu.CompilerParams(vmem_limit_bytes=60 * 1024 * 1024),
        cost_estimate=pl.CostEstimate(flops=0, bytes_accessed=6_000_000, transcendentals=0),
        name="results",
    )(loss, query_grad, table_grad)
    return (loss.reshape(queries), query_grad, table_grad)


def solution(mesh):
    placed = (
        P(("pool", "blk"), None),
        P(("pool", "blk"), None),
        P(),
        P(),
        P(),
        P(("pool", "blk"), None),
        P(("pool", "blk"), None),
        P(("pool", "blk")),
    )
    return jax.shard_map(
        on_device,
        mesh=mesh,
        in_specs=placed,
        out_specs=(P(("pool", "blk")), P(("pool", "blk"), None), P(("pool", "blk"), None)),
        check_vma=False,
    )
```

```python
import functools

import jax
import jax.numpy as jnp
from jax import lax
from jax.experimental import pallas as pl
from jax.experimental.pallas import tpu as pltpu
from jax.sharding import PartitionSpec as P

logit_scale = 80.0
norm_eps = 1e-06
shift = 4.0
log2e = 1.4426950408889634
ln2 = 0.6931471805599453

MESH = pl.DeviceIdType.MESH
f32 = jnp.float32
bf16 = jnp.bfloat16
NN = (((1,), (0,)), ((), ()))
NT = (((1,), (1,)), ((), ()))
TN = (((0,), (0,)), ((), ()))


def mm(a, b, dims=NN):
    return lax.dot_general(a, b, dims, preferred_element_type=f32)


def iota(shape, dim):
    return lax.broadcasted_iota(jnp.int32, shape, dim)


def step_kernel(
    n, nb, group,
    query_hbm, table_hbm, win_hbm, bias_hbm, wout_hbm, rows_hbm, counts_hbm, pos_hbm,
    loss_out, qgrad_out, tgrad_out,
    query_ref, bias_ref, rows_ref, counts_ref, pos_ref, loss_ref, qgrad_ref, table, win, wout, dsilu, tower, item_vec, idx_send, idx_mid, idx_recv, idx_flat, idx_col, idx_row,
    serve, arrive, group_vec, live_col, expo, coef, sums, lossbuf, inv_buf, picked, grad, ret, vg_send, vg_recv,
    row_grad, pre_grad, out_buf,
    a_sem, w_sem, o_sem, isend, irecv, fsend, frecv, bsend, brecv, qsend, qrecv, ssend, srecv, vsend, vrecv,
):
    p = lax.axis_index("pool")
    b = lax.axis_index("blk")
    cap = rows_ref.shape[0]
    slots = n * cap
    span = group * cap
    groups = n // group
    queries, width = query_ref.shape
    chunks, feats, chunk = win.shape
    pool_rows = table.shape[0]
    outs, out_cols = out_buf.shape[0], out_buf.shape[2]

    def load_table():
        return pltpu.make_async_copy(table_hbm, table, w_sem.at[2 * chunks])

    def load_win(c):
        return pltpu.make_async_copy(
            win_hbm.at[:, pl.ds(pl.multiple_of(c * chunk, chunk), chunk)], win.at[c], w_sem.at[c]
        )

    def load_wout(c):
        return pltpu.make_async_copy(
            wout_hbm.at[pl.ds(pl.multiple_of(c * chunk, chunk), chunk), :],
            wout.at[c],
            w_sem.at[chunks + c],
        )

    def ahead(k):
        return lax.rem(p + k, n)

    def behind(k):
        return lax.rem(p + n - k, n)

    planes, plane = idx_recv.shape[0], idx_recv.shape[1]
    my_plane = p // plane
    my_place = lax.rem(p, plane)

    def place_at(k):
        return lax.rem(my_place + k, plane)

    def plane_at(k):
        return lax.rem(my_plane + k, planes)

    def hop1_copy(k):
        other = place_at(k)
        return pltpu.make_async_remote_copy(
            src_ref=idx_send.at[other], dst_ref=idx_mid.at[my_place], send_sem=isend.at[k],
            recv_sem=irecv.at[k], device_id={"pool": my_plane * plane + other},
            device_id_type=MESH,
        )

    def hop1_arrival(k):
        src = place_at(plane - k)
        return pltpu.make_async_remote_copy(
            src_ref=idx_send.at[src], dst_ref=idx_mid.at[src], send_sem=isend.at[k],
            recv_sem=irecv.at[k], device_id={"pool": my_plane * plane + src},
            device_id_type=MESH,
        )

    def hop2_copy(k):
        other = plane_at(k)
        return pltpu.make_async_remote_copy(
            src_ref=idx_mid.at[:, other], dst_ref=idx_recv.at[my_plane],
            send_sem=isend.at[plane + k], recv_sem=irecv.at[plane + k],
            device_id={"pool": other * plane + my_place}, device_id_type=MESH,
        )

    def hop2_arrival(k):
        src = plane_at(planes - k)
        return pltpu.make_async_remote_copy(
            src_ref=idx_mid.at[:, src], dst_ref=idx_recv.at[src],
            send_sem=isend.at[plane + k], recv_sem=irecv.at[plane + k],
            device_id={"pool": src * plane + my_place}, device_id_type=MESH,
        )

    def rows_of(k):
        return pl.ds(pl.multiple_of(k * cap, cap), cap)

    def fwd_copy(k):
        return pltpu.make_async_remote_copy(
            src_ref=serve.at[rows_of(k)], dst_ref=arrive.at[rows_of(k)], send_sem=fsend.at[k],
            recv_sem=frecv.at[k], device_id={"pool": behind(k)}, device_id_type=MESH,
        )

    def bwd_copy(k):
        return pltpu.make_async_remote_copy(
            src_ref=grad.at[rows_of(k)], dst_ref=ret.at[rows_of(k)], send_sem=bsend.at[k],
            recv_sem=brecv.at[k], device_id={"pool": ahead(k)}, device_id_type=MESH,
        )

    def block_of(c):
        return pl.ds(pl.multiple_of(c * queries, queries), queries)

    def query_copy(j):
        return pltpu.make_async_remote_copy(
            src_ref=group_vec.at[block_of(b)], dst_ref=group_vec.at[block_of(b)],
            send_sem=qsend.at[j], recv_sem=qrecv.at[j],
            device_id={"blk": lax.rem(b + j, nb)}, device_id_type=MESH,
        )

    def query_arrival(j):
        src = lax.rem(b + nb - j, nb)
        return pltpu.make_async_remote_copy(
            src_ref=group_vec.at[block_of(src)], dst_ref=group_vec.at[block_of(src)],
            send_sem=qsend.at[j], recv_sem=qrecv.at[j],
            device_id={"blk": lax.rem(b + j, nb)}, device_id_type=MESH,
        )

    def sums_copy(j):
        return pltpu.make_async_remote_copy(
            src_ref=sums.at[b], dst_ref=sums.at[b], send_sem=ssend.at[j], recv_sem=srecv.at[j],
            device_id={"blk": lax.rem(b + j, nb)}, device_id_type=MESH,
        )

    def sums_arrival(j):
        src = lax.rem(b + nb - j, nb)
        return pltpu.make_async_remote_copy(
            src_ref=sums.at[src], dst_ref=sums.at[src], send_sem=ssend.at[j],
            recv_sem=srecv.at[j],
            device_id={"blk": lax.rem(b + j, nb)}, device_id_type=MESH,
        )

    def vg_copy(j):
        return pltpu.make_async_remote_copy(
            src_ref=vg_send.at[j], dst_ref=vg_recv.at[j], send_sem=vsend.at[j],
            recv_sem=vrecv.at[j],
            device_id={"blk": lax.rem(b + j, nb)}, device_id_type=MESH,
        )

    def loop(low, high, body):
        lax.fori_loop(low, high, lambda k, _: (body(k), 0)[1], 0)

    barrier = pltpu.get_barrier_semaphore()

    def greet(device):
        pl.semaphore_signal(barrier, inc=1, device_id=device, device_id_type=MESH)

    loop(1, plane, lambda k: greet({"pool": my_plane * plane + place_at(k)}))
    loop(1, planes, lambda k: greet({"pool": plane_at(k) * plane + my_place}))
    loop(1, nb, lambda j: greet({"blk": lax.rem(b + j, nb)}))

    small = [
        pltpu.make_async_copy(src, dst, a_sem.at[i])
        for i, (src, dst) in enumerate((
            (rows_hbm, rows_ref), (query_hbm, query_ref), (bias_hbm, bias_ref),
            (counts_hbm, counts_ref), (pos_hbm, pos_ref),
        ))
    ]
    for copy in small:
        copy.start()
    load_table().start()
    loop(0, chunks, lambda c: (load_win(c).start(), load_wout(c).start()))

    def parts_of(rows):
        low = lax.rem(rows, 16)
        return (rows - low).astype(f32).astype(bf16), low.astype(f32).astype(bf16)

    small[0].wait()
    turn = (iota((n, n), 0) == iota((n, n), 1)).astype(f32).astype(bf16)
    high, low = parts_of(rows_ref[...])
    idx_flat[...] = jnp.zeros_like(idx_flat)
    idx_flat[:, 0:cap] = (mm(turn, high, NT) + mm(turn, low, NT)).astype(jnp.int32)

    def put_rows(k):
        idx_send[lax.rem(k, plane), k // plane] = idx_flat[pl.ds(k, 1), :]

    loop(0, n, put_rows)

    def tower_chunk(c):
        load_win(c).wait()
        load_wout(c).wait()
        cols = pl.ds(pl.multiple_of(c * chunk, chunk), chunk)
        half = 0.5 * (mm(table[...], win[c]) + bias_ref[:, cols])
        tanh = jnp.tanh(half)
        bent = half * tanh
        tower[...] += mm((half + bent).astype(bf16), wout[c])
        dsilu[c] = ((0.5 + 0.5 * tanh) * (1.0 + (half - bent))).astype(bf16)

    pl.semaphore_wait(barrier, plane + planes + nb - 3)
    loop(1, plane, lambda k: hop1_copy(k).start())
    idx_mid[my_place] = idx_send[my_place]

    small[1].wait()
    query_f = query_ref[...].astype(f32)
    query_inv = lax.rsqrt(jnp.sum(query_f * query_f, axis=1, keepdims=True) + norm_eps)
    group_vec[block_of(b), :] = (query_f * query_inv).astype(bf16)

    tower[...] = jnp.zeros_like(tower)
    small[2].wait()
    load_table().wait()
    loop(0, 1, tower_chunk)
    loop(1, plane, lambda k: hop1_arrival(k).wait_recv())
    loop(1, planes, lambda k: hop2_copy(k).start())

    def own_plane(r):
        idx_recv[my_plane, r] = idx_mid[r, my_plane]

    loop(0, plane, own_plane)
    loop(1, chunks, tower_chunk)

    tower_out = tower[...]
    item_inv = lax.rsqrt(jnp.sum(tower_out * tower_out, axis=1, keepdims=True) + norm_eps)
    item_vec[...] = (tower_out * item_inv).astype(bf16)

    loop(1, planes, lambda k: hop2_arrival(k).wait_recv())

    def flat(k):
        src = behind(k)
        idx_flat[pl.ds(k, 1), :] = idx_recv[src // plane, lax.rem(src, plane)]

    loop(0, n, flat)
    high, low = parts_of(idx_flat[...])
    lanes = idx_flat.shape[1]
    spread = (iota((slots, n), 0) // cap == iota((slots, n), 1)).astype(f32).astype(bf16)
    wide = mm(spread, high) + mm(spread, low)
    idx_col[...] = jnp.sum(
        jnp.where(iota((slots, lanes), 1) == lax.rem(iota((slots, lanes), 0), cap), wide, 0.0),
        axis=1, keepdims=True,
    )
    def span_of(g):
        return pl.ds(pl.multiple_of(g * span, span), span)

    def serve_group(g):
        pick = (
            idx_col[span_of(g), :] == iota((span, pool_rows), 1).astype(f32)
        ).astype(f32).astype(bf16)
        serve[span_of(g), :] = mm(pick, item_vec[...]).astype(bf16)

        def send(i):
            k = g * group + i

            @pl.when(k > 0)
            def _():
                fwd_copy(k).start()

        loop(0, group, send)

        @pl.when(g < nb - 1)
        def _():
            query_copy(g + 1).start()

    loop(0, groups, lambda g: serve_group(lax.rem(g + 1, groups)))
    arrive[rows_of(0), :] = serve[rows_of(0), :]
    spread_t = (iota((n, slots), 1) // cap == iota((n, slots), 0)).astype(f32).astype(bf16)
    tall = mm(high, spread_t, TN) + mm(low, spread_t, TN)
    idx_row[...] = jnp.sum(
        jnp.where(iota((lanes, slots), 0) == lax.rem(iota((lanes, slots), 1), cap), tall, 0.0),
        axis=0, keepdims=True,
    )


    small[3].wait()
    small[4].wait()
    counts = counts_ref[...].astype(f32)
    slot_owner = lax.rem(iota((slots, n), 0) // cap + p, n)
    slot_count = jnp.sum(
        jnp.where(slot_owner == iota((slots, n), 1), counts, 0.0), axis=1, keepdims=True
    )
    live_col[...] = (
        lax.rem(iota((slots, 1), 0), cap).astype(f32) < slot_count
    ).astype(f32)
    own_order = iota((n, n), 0)
    other = iota((n, n), 1)
    ends = jnp.sum(jnp.where(other <= own_order, counts, 0.0), axis=1, keepdims=True)
    count_col = jnp.sum(jnp.where(other == own_order, counts, 0.0), axis=1, keepdims=True)
    pos = pos_ref[...].astype(f32)
    past = ends <= pos
    owner = jnp.sum(jnp.where(past, 1.0, 0.0), axis=0, keepdims=True)
    start = jnp.sum(jnp.where(past, count_col, 0.0), axis=0, keepdims=True)
    owner_rel = lax.rem(owner.astype(jnp.int32) + (n - p), n)
    target = owner_rel * cap + (pos - start).astype(jnp.int32)

    loop(1, nb, lambda j: query_arrival(j).wait_recv())
    all_queries = nb * queries
    sums[b] = jnp.zeros((1, all_queries), f32)
    picked[...] = jnp.zeros_like(picked)

    def hits(g):
        return iota((span, queries), 0) + g * span == target

    def score_group(g):
        def arrival(i):
            k = g * group + i

            @pl.when(k > 0)
            def _():
                fwd_copy(k).wait_recv()

        loop(0, group, arrival)
        vecs = arrive[span_of(g), :]
        scores = mm(vecs, group_vec[...], NT)
        part = jnp.exp2(scores * (logit_scale * log2e) - shift) * live_col[span_of(g), :]
        expo[span_of(g), :] = part
        sums[b] = sums[b] + jnp.sum(part, axis=0, keepdims=True)
        own = mm(vecs, group_vec[block_of(b), :], NT)
        picked[...] += jnp.sum(jnp.where(hits(g), own, 0.0), axis=0, keepdims=True)

    loop(0, groups, lambda g: score_group(lax.rem(g * 3, groups)))
    loop(1, nb, lambda j: sums_copy(j).start())
    loop(1, nb, lambda j: sums_arrival(j).wait_recv())
    total = sums[0]
    for j in range(1, nb):
        total = total + sums[j]
    inv_total = 1.0 / total
    inv_buf[...] = inv_total
    lossbuf[...] = jnp.log(total) + shift * ln2
    loss_ref[...] = lossbuf[:, block_of(b)] - logit_scale * picked[...]
    loss_copy = pltpu.make_async_copy(loss_ref, loss_out, o_sem.at[outs])
    loss_copy.start()

    def coef_group(g):
        coef[span_of(g), :] = (expo[span_of(g), :] * inv_total).astype(bf16)
        coef[span_of(g), block_of(b)] = (
            expo[span_of(g), block_of(b)] * inv_buf[:, block_of(b)] - jnp.where(hits(g), 1.0, 0.0)
        ).astype(bf16)
        grad[span_of(g), :] = (logit_scale * mm(coef[span_of(g), :], group_vec[...])).astype(bf16)

        def send(i):
            k = g * group + i

            @pl.when(k > 0)
            def _():
                bwd_copy(k).start()

        loop(0, group, send)

    loop(0, groups, lambda g: coef_group(lax.rem(g + 1, groups)))
    ret[rows_of(0), :] = grad[rows_of(0), :]

    def part_of(c):
        return logit_scale * mm(coef[:, block_of(c)], arrive[...], TN)

    def send_part(j):
        vg_send[j] = part_of(lax.rem(b + j, nb)).astype(bf16)
        vg_copy(j).start()

    loop(1, nb, send_part)
    vec_grad = part_of(b)
    loop(1, plane, lambda k: hop1_copy(k).wait_send())
    loop(1, planes, lambda k: hop2_copy(k).wait_send())
    loop(1, n, lambda k: fwd_copy(k).wait_send())
    loop(1, nb, lambda j: (query_copy(j).wait_send(), sums_copy(j).wait_send()))

    row_grad[...] = jnp.zeros_like(row_grad)

    def sum_group(g):
        def arrival(i):
            k = g * group + i

            @pl.when(k > 0)
            def _():
                bwd_copy(k).wait_recv()

        loop(0, group, arrival)
        pick_t = (
            iota((pool_rows, span), 0).astype(f32) == idx_row[:, span_of(g)]
        ).astype(f32).astype(bf16)
        row_grad[...] += mm(pick_t, ret[span_of(g), :])

    loop(0, groups // 2, lambda g: sum_group(lax.rem(g * 3, groups)))
    loop(1, nb, lambda j: vg_copy(j).wait_recv())
    for j in range(1, nb):
        vec_grad = vec_grad + vg_recv[j].astype(f32)
    query_f = query_ref[...].astype(f32)
    qgrad_ref[...] = vec_grad * query_inv - query_f * (query_inv * query_inv * query_inv) * jnp.sum(
        query_f * vec_grad, axis=1, keepdims=True
    )
    qgrad_copy = pltpu.make_async_copy(qgrad_ref, qgrad_out, o_sem.at[outs + 1])
    qgrad_copy.start()
    loop(groups // 2, groups, lambda g: sum_group(lax.rem(g * 3, groups)))

    tower_out = tower[...]
    item_inv = lax.rsqrt(jnp.sum(tower_out * tower_out, axis=1, keepdims=True) + norm_eps)
    summed = row_grad[...]
    item_vec[...] = (
        summed * item_inv
        - tower_out * (item_inv * item_inv * item_inv)
        * jnp.sum(tower_out * summed, axis=1, keepdims=True)
    ).astype(bf16)

    def back_chunk(c):
        pre_grad[c] = (mm(item_vec[...], wout[c], NT) * dsilu[c].astype(f32)).astype(bf16)

    loop(0, chunks, back_chunk)

    def out_copy(f):
        return pltpu.make_async_copy(
            out_buf.at[f],
            tgrad_out.at[:, pl.ds(pl.multiple_of(f * out_cols, out_cols), out_cols)],
            o_sem.at[f],
        )

    def out_block(f):
        rows = pl.ds(pl.multiple_of(f * out_cols, out_cols), out_cols)
        total = mm(pre_grad[0], win[0, rows, :], NT)
        for c in range(1, chunks):
            total = total + mm(pre_grad[c], win[c, rows, :], NT)
        out_buf[f] = total
        out_copy(f).start()

    if outs % 2:
        loop(0, outs, out_block)
    else:
        loop(0, outs // 2, lambda i: (out_block(2 * i), out_block(2 * i + 1)))

    loop(1, n, lambda k: bwd_copy(k).wait_send())
    loop(1, nb, lambda j: vg_copy(j).wait_send())
    loss_copy.wait()
    qgrad_copy.wait()
    loop(0, outs, lambda f: out_copy(f).wait())


def copy_kernel(
    loss_in, qgrad_in, tgrad_in, loss_out, qgrad_out, tgrad_out, loss_ref, qgrad_ref, tgrad_ref,
    in_sem, out_sem
):
    parts = out_sem.shape[0] - 2
    rows = tgrad_ref.shape[0] // parts
    moves = [
        (tgrad_in.at[pl.ds(i * rows, rows)], tgrad_ref.at[pl.ds(i * rows, rows)],
         tgrad_out.at[pl.ds(i * rows, rows)])
        for i in range(parts)
    ]
    moves += [(qgrad_in, qgrad_ref, qgrad_out), (loss_in, loss_ref, loss_out)]
    loads = [
        pltpu.make_async_copy(src, mid, in_sem.at[i]) for i, (src, mid, _) in enumerate(moves)
    ]
    saves = [
        pltpu.make_async_copy(mid, dst, out_sem.at[i]) for i, (_, mid, dst) in enumerate(moves)
    ]
    for load in loads:
        load.start()
    for load, save in zip(loads, saves):
        load.wait()
        save.start()
    for save in saves:
        save.wait()


def on_device(query_emb, item_table, w_in, bias_in, w_out, fetch_rows, fetch_counts, pos_slot):
    n = lax.axis_size("pool")
    nb = lax.axis_size("blk")
    cap = fetch_rows.shape[1]
    slots = n * cap
    queries, width = query_emb.shape
    pool_rows, feats = item_table.shape
    hid = w_in.shape[1]
    chunk = min(1024, hid)
    chunks = hid // chunk
    group = min(16, n // 2)
    plane = 8 if n % 8 == 0 and n > 8 else 2
    out_cols = min(256, feats)
    outs = feats // out_cols
    every = nb * queries
    in_hbm = pl.BlockSpec(memory_space=pltpu.HBM)
    dma = pltpu.SemaphoreType.DMA
    flops = 2 * pool_rows * hid * (feats + width) * 2 + 6 * slots * every * width
    loss, query_grad, table_grad = pl.pallas_call(
        functools.partial(step_kernel, n, nb, group),
        out_shape=(
            jax.ShapeDtypeStruct((1, queries), f32),
            jax.ShapeDtypeStruct((queries, width), f32),
            jax.ShapeDtypeStruct((pool_rows, feats), f32),
        ),
        in_specs=[in_hbm] * 8,
        out_specs=(in_hbm, in_hbm, in_hbm),
        scratch_shapes=[
            pltpu.VMEM((queries, width), bf16),
            pltpu.VMEM((1, hid), f32),
            pltpu.VMEM((cap, n), jnp.int32),
            pltpu.VMEM((1, n), jnp.int32),
            pltpu.VMEM((1, queries), jnp.int32),
            pltpu.VMEM((1, queries), f32),
            pltpu.VMEM((queries, width), f32),
            pltpu.VMEM((pool_rows, feats), bf16),
            pltpu.VMEM((chunks, feats, chunk), bf16),
            pltpu.VMEM((chunks, chunk, width), bf16),
            pltpu.VMEM((chunks, pool_rows, chunk), bf16),
            pltpu.VMEM((pool_rows, width), f32),
            pltpu.VMEM((pool_rows, width), bf16),
            pltpu.VMEM((plane, n // plane, 1, 128), jnp.int32),
            pltpu.VMEM((plane, n // plane, 1, 128), jnp.int32),
            pltpu.VMEM((n // plane, plane, 1, 128), jnp.int32),
            pltpu.VMEM((n, 128), jnp.int32),
            pltpu.VMEM((slots, 1), f32),
            pltpu.VMEM((1, slots), f32),
            pltpu.VMEM((slots, width), bf16),
            pltpu.VMEM((slots, width), bf16),
            pltpu.VMEM((every, width), bf16),
            pltpu.VMEM((slots, 1), f32),
            pltpu.VMEM((slots, every), f32),
            pltpu.VMEM((slots, every), bf16),
            pltpu.VMEM((nb, 1, every), f32),
            pltpu.VMEM((1, every), f32),
            pltpu.VMEM((1, every), f32),
            pltpu.VMEM((1, queries), f32),
            pltpu.VMEM((slots, width), bf16),
            pltpu.VMEM((slots, width), bf16),
            pltpu.VMEM((nb, queries, width), bf16),
            pltpu.VMEM((nb, queries, width), bf16),
            pltpu.VMEM((pool_rows, width), f32),
            pltpu.VMEM((chunks, pool_rows, chunk), bf16),
            pltpu.VMEM((outs, pool_rows, out_cols), f32),
            dma((5,)),
            dma((2 * chunks + 1,)),
            dma((outs + 2,)),
            dma((plane + n // plane,)), dma((plane + n // plane,)),
            dma((n,)), dma((n,)), dma((n,)), dma((n,)),
            dma((nb,)), dma((nb,)), dma((nb,)), dma((nb,)), dma((nb,)), dma((nb,)),
        ],
        compiler_params=pltpu.CompilerParams(
            collective_id=0, has_side_effects=True, vmem_limit_bytes=60 * 1024 * 1024
        ),
        cost_estimate=pl.CostEstimate(
            flops=flops, bytes_accessed=20_000_000, transcendentals=3_000_000
        ),
        name="retrieval_step",
    )(
        query_emb, item_table, w_in, bias_in.reshape(1, hid), w_out, fetch_rows.T, fetch_counts,
        pos_slot.reshape(1, queries),
    )
    parts = 4
    loss, query_grad, table_grad = pl.pallas_call(
        copy_kernel,
        out_shape=(
            jax.ShapeDtypeStruct((1, queries), f32),
            jax.ShapeDtypeStruct((queries, width), f32),
            jax.ShapeDtypeStruct((pool_rows, feats), f32),
        ),
        in_specs=[in_hbm] * 3,
        out_specs=(in_hbm, in_hbm, in_hbm),
        scratch_shapes=[
            pltpu.VMEM((1, queries), f32),
            pltpu.VMEM((queries, width), f32),
            pltpu.VMEM((pool_rows, feats), f32),
            dma((parts + 2,)),
            dma((parts + 2,)),
        ],
        compiler_params=pltpu.CompilerParams(vmem_limit_bytes=60 * 1024 * 1024),
        cost_estimate=pl.CostEstimate(flops=0, bytes_accessed=6_000_000, transcendentals=0),
        name="results",
    )(loss, query_grad, table_grad)
    return (loss.reshape(queries), query_grad, table_grad)


def solution(mesh):
    placed = (
        P(("pool", "blk"), None),
        P(("pool", "blk"), None),
        P(),
        P(),
        P(),
        P(("pool", "blk"), None),
        P(("pool", "blk"), None),
        P(("pool", "blk")),
    )
    return jax.shard_map(
        on_device,
        mesh=mesh,
        in_specs=placed,
        out_specs=(P(("pool", "blk")), P(("pool", "blk"), None), P(("pool", "blk"), None)),
        check_vma=False,
    )
```

```python
import functools

import jax
import jax.numpy as jnp
from jax import lax
from jax.experimental import pallas as pl
from jax.experimental.pallas import tpu as pltpu
from jax.sharding import PartitionSpec as P

logit_scale = 80.0
norm_eps = 1e-06
shift = 4.0
log2e = 1.4426950408889634
ln2 = 0.6931471805599453

MESH = pl.DeviceIdType.MESH
f32 = jnp.float32
bf16 = jnp.bfloat16
NN = (((1,), (0,)), ((), ()))
NT = (((1,), (1,)), ((), ()))
TN = (((0,), (0,)), ((), ()))


def mm(a, b, dims=NN):
    return lax.dot_general(a, b, dims, preferred_element_type=f32)


def iota(shape, dim):
    return lax.broadcasted_iota(jnp.int32, shape, dim)


def step_kernel(
    n, nb, group,
    query_hbm, table_hbm, win_hbm, bias_hbm, wout_hbm, rows_hbm, counts_hbm, pos_hbm,
    loss_out, qgrad_out, tgrad_out,
    query_ref, bias_ref, rows_ref, counts_ref, pos_ref, loss_ref, qgrad_ref, table, win, wout, dsilu, tower, item_vec, idx_send, idx_mid, idx_recv, idx_flat, idx_col, idx_row,
    serve, arrive, group_vec, inv_col, live_col, expo, coef, sums, lossbuf, inv_buf, picked, grad, ret, vg_send, vg_recv,
    row_grad, pre_grad, out_buf,
    a_sem, w_sem, o_sem, isend, irecv, fsend, frecv, bsend, brecv, qsend, qrecv, ssend, srecv, vsend, vrecv,
):
    p = lax.axis_index("pool")
    b = lax.axis_index("blk")
    cap = rows_ref.shape[0]
    slots = n * cap
    span = group * cap
    groups = n // group
    queries, width = query_ref.shape
    chunks, feats, chunk = win.shape
    pool_rows = table.shape[0]
    outs, out_cols = out_buf.shape[0], out_buf.shape[2]

    def load_table():
        return pltpu.make_async_copy(table_hbm, table, w_sem.at[2 * chunks])

    def load_win(c):
        return pltpu.make_async_copy(
            win_hbm.at[:, pl.ds(pl.multiple_of(c * chunk, chunk), chunk)], win.at[c], w_sem.at[c]
        )

    def load_wout(c):
        return pltpu.make_async_copy(
            wout_hbm.at[pl.ds(pl.multiple_of(c * chunk, chunk), chunk), :],
            wout.at[c],
            w_sem.at[chunks + c],
        )

    def ahead(k):
        return lax.rem(p + k, n)

    def behind(k):
        return lax.rem(p + n - k, n)

    planes, plane = idx_recv.shape[0], idx_recv.shape[1]
    my_plane = p // plane
    my_place = lax.rem(p, plane)

    def place_at(k):
        return lax.rem(my_place + k, plane)

    def plane_at(k):
        return lax.rem(my_plane + k, planes)

    def hop1_copy(k):
        other = place_at(k)
        return pltpu.make_async_remote_copy(
            src_ref=idx_send.at[other], dst_ref=idx_mid.at[my_place], send_sem=isend.at[k],
            recv_sem=irecv.at[k], device_id={"pool": my_plane * plane + other},
            device_id_type=MESH,
        )

    def hop1_arrival(k):
        src = place_at(plane - k)
        return pltpu.make_async_remote_copy(
            src_ref=idx_send.at[src], dst_ref=idx_mid.at[src], send_sem=isend.at[k],
            recv_sem=irecv.at[k], device_id={"pool": my_plane * plane + src},
            device_id_type=MESH,
        )

    def hop2_copy(k):
        other = plane_at(k)
        return pltpu.make_async_remote_copy(
            src_ref=idx_mid.at[:, other], dst_ref=idx_recv.at[my_plane],
            send_sem=isend.at[plane + k], recv_sem=irecv.at[plane + k],
            device_id={"pool": other * plane + my_place}, device_id_type=MESH,
        )

    def hop2_arrival(k):
        src = plane_at(planes - k)
        return pltpu.make_async_remote_copy(
            src_ref=idx_mid.at[:, src], dst_ref=idx_recv.at[src],
            send_sem=isend.at[plane + k], recv_sem=irecv.at[plane + k],
            device_id={"pool": src * plane + my_place}, device_id_type=MESH,
        )

    def rows_of(k):
        return pl.ds(pl.multiple_of(k * cap, cap), cap)

    def fwd_copy(k):
        return pltpu.make_async_remote_copy(
            src_ref=serve.at[rows_of(k)], dst_ref=arrive.at[rows_of(k)], send_sem=fsend.at[k],
            recv_sem=frecv.at[k], device_id={"pool": behind(k)}, device_id_type=MESH,
        )

    def bwd_copy(k):
        return pltpu.make_async_remote_copy(
            src_ref=grad.at[rows_of(k)], dst_ref=ret.at[rows_of(k)], send_sem=bsend.at[k],
            recv_sem=brecv.at[k], device_id={"pool": ahead(k)}, device_id_type=MESH,
        )

    def block_of(c):
        return pl.ds(pl.multiple_of(c * queries, queries), queries)

    def query_copy(j):
        return pltpu.make_async_remote_copy(
            src_ref=group_vec.at[block_of(b)], dst_ref=group_vec.at[block_of(b)],
            send_sem=qsend.at[j], recv_sem=qrecv.at[j],
            device_id={"blk": lax.rem(b + j, nb)}, device_id_type=MESH,
        )

    def query_arrival(j):
        src = lax.rem(b + nb - j, nb)
        return pltpu.make_async_remote_copy(
            src_ref=group_vec.at[block_of(src)], dst_ref=group_vec.at[block_of(src)],
            send_sem=qsend.at[j], recv_sem=qrecv.at[j],
            device_id={"blk": lax.rem(b + j, nb)}, device_id_type=MESH,
        )

    def sums_copy(j):
        return pltpu.make_async_remote_copy(
            src_ref=sums.at[b], dst_ref=sums.at[b], send_sem=ssend.at[j], recv_sem=srecv.at[j],
            device_id={"blk": lax.rem(b + j, nb)}, device_id_type=MESH,
        )

    def sums_arrival(j):
        src = lax.rem(b + nb - j, nb)
        return pltpu.make_async_remote_copy(
            src_ref=sums.at[src], dst_ref=sums.at[src], send_sem=ssend.at[j],
            recv_sem=srecv.at[j],
            device_id={"blk": lax.rem(b + j, nb)}, device_id_type=MESH,
        )

    def vg_copy(j):
        return pltpu.make_async_remote_copy(
            src_ref=vg_send.at[j], dst_ref=vg_recv.at[j], send_sem=vsend.at[j],
            recv_sem=vrecv.at[j],
            device_id={"blk": lax.rem(b + j, nb)}, device_id_type=MESH,
        )

    def loop(low, high, body):
        lax.fori_loop(low, high, lambda k, _: (body(k), 0)[1], 0)

    barrier = pltpu.get_barrier_semaphore()

    def greet(device):
        pl.semaphore_signal(barrier, inc=1, device_id=device, device_id_type=MESH)

    loop(1, plane, lambda k: greet({"pool": my_plane * plane + place_at(k)}))
    loop(1, planes, lambda k: greet({"pool": plane_at(k) * plane + my_place}))
    loop(1, nb, lambda j: greet({"blk": lax.rem(b + j, nb)}))

    small = [
        pltpu.make_async_copy(src, dst, a_sem.at[i])
        for i, (src, dst) in enumerate((
            (rows_hbm, rows_ref), (query_hbm, query_ref), (bias_hbm, bias_ref),
            (counts_hbm, counts_ref), (pos_hbm, pos_ref),
        ))
    ]
    for copy in small:
        copy.start()
    load_table().start()
    loop(0, chunks, lambda c: (load_win(c).start(), load_wout(c).start()))

    def parts_of(rows):
        low = lax.rem(rows, 16)
        return (rows - low).astype(f32).astype(bf16), low.astype(f32).astype(bf16)

    small[0].wait()
    turn = (iota((n, n), 0) == iota((n, n), 1)).astype(f32).astype(bf16)
    high, low = parts_of(rows_ref[...])
    idx_flat[...] = jnp.zeros_like(idx_flat)
    idx_flat[:, 0:cap] = (mm(turn, high, NT) + mm(turn, low, NT)).astype(jnp.int32)

    def put_rows(k):
        idx_send[lax.rem(k, plane), k // plane] = idx_flat[pl.ds(k, 1), :]

    loop(0, n, put_rows)

    def tower_chunk(c):
        load_win(c).wait()
        load_wout(c).wait()
        cols = pl.ds(pl.multiple_of(c * chunk, chunk), chunk)
        half = 0.5 * (mm(table[...], win[c]) + bias_ref[:, cols])
        tanh = jnp.tanh(half)
        bent = half * tanh
        tower[...] += mm((half + bent).astype(bf16), wout[c])
        dsilu[c] = ((0.5 + 0.5 * tanh) * (1.0 + (half - bent))).astype(bf16)

    pl.semaphore_wait(barrier, plane + planes + nb - 3)
    loop(1, plane, lambda k: hop1_copy(k).start())
    idx_mid[my_place] = idx_send[my_place]

    small[1].wait()
    query_f = query_ref[...].astype(f32)
    query_inv = lax.rsqrt(jnp.sum(query_f * query_f, axis=1, keepdims=True) + norm_eps)
    group_vec[block_of(b), :] = (query_f * query_inv).astype(bf16)

    tower[...] = jnp.zeros_like(tower)
    small[2].wait()
    load_table().wait()
    loop(0, 1, tower_chunk)
    loop(1, plane, lambda k: hop1_arrival(k).wait_recv())
    loop(1, planes, lambda k: hop2_copy(k).start())

    def own_plane(r):
        idx_recv[my_plane, r] = idx_mid[r, my_plane]

    loop(0, plane, own_plane)
    loop(1, chunks, tower_chunk)

    tower_out = tower[...]
    item_inv = lax.rsqrt(jnp.sum(tower_out * tower_out, axis=1, keepdims=True) + norm_eps)
    inv_col[...] = item_inv
    item_vec[...] = (tower_out * item_inv).astype(bf16)

    loop(1, planes, lambda k: hop2_arrival(k).wait_recv())

    def flat(k):
        src = behind(k)
        idx_flat[pl.ds(k, 1), :] = idx_recv[src // plane, lax.rem(src, plane)]

    loop(0, n, flat)
    high, low = parts_of(idx_flat[...])
    lanes = idx_flat.shape[1]
    spread = (iota((slots, n), 0) // cap == iota((slots, n), 1)).astype(f32).astype(bf16)
    wide = mm(spread, high) + mm(spread, low)
    idx_col[...] = jnp.sum(
        jnp.where(iota((slots, lanes), 1) == lax.rem(iota((slots, lanes), 0), cap), wide, 0.0),
        axis=1, keepdims=True,
    )
    def span_of(g):
        return pl.ds(pl.multiple_of(g * span, span), span)

    def serve_group(g):
        pick = (
            idx_col[span_of(g), :] == iota((span, pool_rows), 1).astype(f32)
        ).astype(f32).astype(bf16)
        serve[span_of(g), :] = mm(pick, item_vec[...]).astype(bf16)

        def send(i):
            k = g * group + i

            @pl.when(k > 0)
            def _():
                fwd_copy(k).start()

        loop(0, group, send)

        @pl.when(g < nb - 1)
        def _():
            query_copy(g + 1).start()

    loop(0, groups, lambda g: serve_group(lax.rem(g + 1, groups)))
    arrive[rows_of(0), :] = serve[rows_of(0), :]
    spread_t = (iota((n, slots), 1) // cap == iota((n, slots), 0)).astype(f32).astype(bf16)
    tall = mm(high, spread_t, TN) + mm(low, spread_t, TN)
    idx_row[...] = jnp.sum(
        jnp.where(iota((lanes, slots), 0) == lax.rem(iota((lanes, slots), 1), cap), tall, 0.0),
        axis=0, keepdims=True,
    )


    small[3].wait()
    small[4].wait()
    counts = counts_ref[...].astype(f32)
    slot_owner = lax.rem(iota((slots, n), 0) // cap + p, n)
    slot_count = jnp.sum(
        jnp.where(slot_owner == iota((slots, n), 1), counts, 0.0), axis=1, keepdims=True
    )
    live_col[...] = (
        lax.rem(iota((slots, 1), 0), cap).astype(f32) < slot_count
    ).astype(f32)
    own_order = iota((n, n), 0)
    other = iota((n, n), 1)
    ends = jnp.sum(jnp.where(other <= own_order, counts, 0.0), axis=1, keepdims=True)
    count_col = jnp.sum(jnp.where(other == own_order, counts, 0.0), axis=1, keepdims=True)
    pos = pos_ref[...].astype(f32)
    past = ends <= pos
    owner = jnp.sum(jnp.where(past, 1.0, 0.0), axis=0, keepdims=True)
    start = jnp.sum(jnp.where(past, count_col, 0.0), axis=0, keepdims=True)
    owner_rel = lax.rem(owner.astype(jnp.int32) + (n - p), n)
    target = owner_rel * cap + (pos - start).astype(jnp.int32)

    loop(1, nb, lambda j: query_arrival(j).wait_recv())
    all_queries = nb * queries
    sums[b] = jnp.zeros((1, all_queries), f32)
    picked[...] = jnp.zeros_like(picked)

    def hits(g):
        return iota((span, queries), 0) + g * span == target

    def score_group(g):
        def arrival(i):
            k = g * group + i

            @pl.when(k > 0)
            def _():
                fwd_copy(k).wait_recv()

        loop(0, group, arrival)
        vecs = arrive[span_of(g), :]
        scores = mm(vecs, group_vec[...], NT)
        part = jnp.exp2(scores * (logit_scale * log2e) - shift) * live_col[span_of(g), :]
        expo[span_of(g), :] = part
        sums[b] = sums[b] + jnp.sum(part, axis=0, keepdims=True)
        own = mm(vecs, group_vec[block_of(b), :], NT)
        picked[...] += jnp.sum(jnp.where(hits(g), own, 0.0), axis=0, keepdims=True)

    loop(0, groups, lambda g: score_group(lax.rem(g * 3, groups)))
    loop(1, nb, lambda j: sums_copy(j).start())
    loop(1, nb, lambda j: sums_arrival(j).wait_recv())
    total = sums[0]
    for j in range(1, nb):
        total = total + sums[j]
    inv_total = 1.0 / total
    inv_buf[...] = inv_total
    lossbuf[...] = jnp.log(total) + shift * ln2
    loss_ref[...] = lossbuf[:, block_of(b)] - logit_scale * picked[...]
    loss_copy = pltpu.make_async_copy(loss_ref, loss_out, o_sem.at[outs])
    loss_copy.start()

    def coef_group(g):
        coef[span_of(g), :] = (expo[span_of(g), :] * inv_total).astype(bf16)
        coef[span_of(g), block_of(b)] = (
            expo[span_of(g), block_of(b)] * inv_buf[:, block_of(b)] - jnp.where(hits(g), 1.0, 0.0)
        ).astype(bf16)
        grad[span_of(g), :] = (logit_scale * mm(coef[span_of(g), :], group_vec[...])).astype(bf16)

        def send(i):
            k = g * group + i

            @pl.when(k > 0)
            def _():
                bwd_copy(k).start()

        loop(0, group, send)

    loop(0, groups, lambda g: coef_group(lax.rem(g + 1, groups)))
    ret[rows_of(0), :] = grad[rows_of(0), :]

    def part_of(c):
        return logit_scale * mm(coef[:, block_of(c)], arrive[...], TN)

    def send_part(j):
        vg_send[j] = part_of(lax.rem(b + j, nb)).astype(bf16)
        vg_copy(j).start()

    loop(1, nb, send_part)
    vec_grad = part_of(b)
    tower[...] = tower[...] * inv_col[...]
    loop(1, plane, lambda k: hop1_copy(k).wait_send())
    loop(1, planes, lambda k: hop2_copy(k).wait_send())
    loop(1, n, lambda k: fwd_copy(k).wait_send())
    loop(1, nb, lambda j: (query_copy(j).wait_send(), sums_copy(j).wait_send()))

    row_grad[...] = jnp.zeros_like(row_grad)

    def sum_group(g):
        def arrival(i):
            k = g * group + i

            @pl.when(k > 0)
            def _():
                bwd_copy(k).wait_recv()

        loop(0, group, arrival)
        pick_t = (
            iota((pool_rows, span), 0).astype(f32) == idx_row[:, span_of(g)]
        ).astype(f32).astype(bf16)
        row_grad[...] += mm(pick_t, ret[span_of(g), :])

    loop(0, groups // 2, lambda g: sum_group(lax.rem(g * 3, groups)))
    loop(1, nb, lambda j: vg_copy(j).wait_recv())
    for j in range(1, nb):
        vec_grad = vec_grad + vg_recv[j].astype(f32)
    query_f = query_ref[...].astype(f32)
    qgrad_ref[...] = vec_grad * query_inv - query_f * (query_inv * query_inv * query_inv) * jnp.sum(
        query_f * vec_grad, axis=1, keepdims=True
    )
    qgrad_copy = pltpu.make_async_copy(qgrad_ref, qgrad_out, o_sem.at[outs + 1])
    qgrad_copy.start()
    loop(groups // 2, groups, lambda g: sum_group(lax.rem(g * 3, groups)))

    summed = row_grad[...]
    unit = tower[...]
    item_vec[...] = (
        inv_col[...] * (summed - unit * jnp.sum(unit * summed, axis=1, keepdims=True))
    ).astype(bf16)

    def back_chunk(c):
        pre_grad[c] = (mm(item_vec[...], wout[c], NT) * dsilu[c].astype(f32)).astype(bf16)

    loop(0, chunks, back_chunk)

    def out_copy(f):
        return pltpu.make_async_copy(
            out_buf.at[f],
            tgrad_out.at[:, pl.ds(pl.multiple_of(f * out_cols, out_cols), out_cols)],
            o_sem.at[f],
        )

    def out_block(f):
        rows = pl.ds(pl.multiple_of(f * out_cols, out_cols), out_cols)
        total = mm(pre_grad[0], win[0, rows, :], NT)
        for c in range(1, chunks):
            total = total + mm(pre_grad[c], win[c, rows, :], NT)
        out_buf[f] = total
        out_copy(f).start()

    if outs % 2:
        loop(0, outs, out_block)
    else:
        loop(0, outs // 2, lambda i: (out_block(2 * i), out_block(2 * i + 1)))

    loop(1, n, lambda k: bwd_copy(k).wait_send())
    loop(1, nb, lambda j: vg_copy(j).wait_send())
    loss_copy.wait()
    qgrad_copy.wait()
    loop(0, outs, lambda f: out_copy(f).wait())


def copy_kernel(
    loss_in, qgrad_in, tgrad_in, loss_out, qgrad_out, tgrad_out, loss_ref, qgrad_ref, tgrad_ref,
    in_sem, out_sem
):
    parts = out_sem.shape[0] - 2
    rows = tgrad_ref.shape[0] // parts
    moves = [
        (tgrad_in.at[pl.ds(i * rows, rows)], tgrad_ref.at[pl.ds(i * rows, rows)],
         tgrad_out.at[pl.ds(i * rows, rows)])
        for i in range(parts)
    ]
    moves += [(qgrad_in, qgrad_ref, qgrad_out), (loss_in, loss_ref, loss_out)]
    loads = [
        pltpu.make_async_copy(src, mid, in_sem.at[i]) for i, (src, mid, _) in enumerate(moves)
    ]
    saves = [
        pltpu.make_async_copy(mid, dst, out_sem.at[i]) for i, (_, mid, dst) in enumerate(moves)
    ]
    for load in loads:
        load.start()
    for load, save in zip(loads, saves):
        load.wait()
        save.start()
    for save in saves:
        save.wait()


def on_device(query_emb, item_table, w_in, bias_in, w_out, fetch_rows, fetch_counts, pos_slot):
    n = lax.axis_size("pool")
    nb = lax.axis_size("blk")
    cap = fetch_rows.shape[1]
    slots = n * cap
    queries, width = query_emb.shape
    pool_rows, feats = item_table.shape
    hid = w_in.shape[1]
    chunk = min(1024, hid)
    chunks = hid // chunk
    group = min(16, n // 2)
    plane = 8 if n % 8 == 0 and n > 8 else 2
    out_cols = min(256, feats)
    outs = feats // out_cols
    every = nb * queries
    in_hbm = pl.BlockSpec(memory_space=pltpu.HBM)
    dma = pltpu.SemaphoreType.DMA
    flops = 2 * pool_rows * hid * (feats + width) * 2 + 6 * slots * every * width
    loss, query_grad, table_grad = pl.pallas_call(
        functools.partial(step_kernel, n, nb, group),
        out_shape=(
            jax.ShapeDtypeStruct((1, queries), f32),
            jax.ShapeDtypeStruct((queries, width), f32),
            jax.ShapeDtypeStruct((pool_rows, feats), f32),
        ),
        in_specs=[in_hbm] * 8,
        out_specs=(in_hbm, in_hbm, in_hbm),
        scratch_shapes=[
            pltpu.VMEM((queries, width), bf16),
            pltpu.VMEM((1, hid), f32),
            pltpu.VMEM((cap, n), jnp.int32),
            pltpu.VMEM((1, n), jnp.int32),
            pltpu.VMEM((1, queries), jnp.int32),
            pltpu.VMEM((1, queries), f32),
            pltpu.VMEM((queries, width), f32),
            pltpu.VMEM((pool_rows, feats), bf16),
            pltpu.VMEM((chunks, feats, chunk), bf16),
            pltpu.VMEM((chunks, chunk, width), bf16),
            pltpu.VMEM((chunks, pool_rows, chunk), bf16),
            pltpu.VMEM((pool_rows, width), f32),
            pltpu.VMEM((pool_rows, width), bf16),
            pltpu.VMEM((plane, n // plane, 1, 128), jnp.int32),
            pltpu.VMEM((plane, n // plane, 1, 128), jnp.int32),
            pltpu.VMEM((n // plane, plane, 1, 128), jnp.int32),
            pltpu.VMEM((n, 128), jnp.int32),
            pltpu.VMEM((slots, 1), f32),
            pltpu.VMEM((1, slots), f32),
            pltpu.VMEM((slots, width), bf16),
            pltpu.VMEM((slots, width), bf16),
            pltpu.VMEM((every, width), bf16),
            pltpu.VMEM((pool_rows, 1), f32),
            pltpu.VMEM((slots, 1), f32),
            pltpu.VMEM((slots, every), f32),
            pltpu.VMEM((slots, every), bf16),
            pltpu.VMEM((nb, 1, every), f32),
            pltpu.VMEM((1, every), f32),
            pltpu.VMEM((1, every), f32),
            pltpu.VMEM((1, queries), f32),
            pltpu.VMEM((slots, width), bf16),
            pltpu.VMEM((slots, width), bf16),
            pltpu.VMEM((nb, queries, width), bf16),
            pltpu.VMEM((nb, queries, width), bf16),
            pltpu.VMEM((pool_rows, width), f32),
            pltpu.VMEM((chunks, pool_rows, chunk), bf16),
            pltpu.VMEM((outs, pool_rows, out_cols), f32),
            dma((5,)),
            dma((2 * chunks + 1,)),
            dma((outs + 2,)),
            dma((plane + n // plane,)), dma((plane + n // plane,)),
            dma((n,)), dma((n,)), dma((n,)), dma((n,)),
            dma((nb,)), dma((nb,)), dma((nb,)), dma((nb,)), dma((nb,)), dma((nb,)),
        ],
        compiler_params=pltpu.CompilerParams(
            collective_id=0, has_side_effects=True, vmem_limit_bytes=60 * 1024 * 1024
        ),
        cost_estimate=pl.CostEstimate(
            flops=flops, bytes_accessed=20_000_000, transcendentals=3_000_000
        ),
        name="retrieval_step",
    )(
        query_emb, item_table, w_in, bias_in.reshape(1, hid), w_out, fetch_rows.T, fetch_counts,
        pos_slot.reshape(1, queries),
    )
    parts = 4
    loss, query_grad, table_grad = pl.pallas_call(
        copy_kernel,
        out_shape=(
            jax.ShapeDtypeStruct((1, queries), f32),
            jax.ShapeDtypeStruct((queries, width), f32),
            jax.ShapeDtypeStruct((pool_rows, feats), f32),
        ),
        in_specs=[in_hbm] * 3,
        out_specs=(in_hbm, in_hbm, in_hbm),
        scratch_shapes=[
            pltpu.VMEM((1, queries), f32),
            pltpu.VMEM((queries, width), f32),
            pltpu.VMEM((pool_rows, feats), f32),
            dma((parts + 2,)),
            dma((parts + 2,)),
        ],
        compiler_params=pltpu.CompilerParams(vmem_limit_bytes=60 * 1024 * 1024),
        cost_estimate=pl.CostEstimate(flops=0, bytes_accessed=6_000_000, transcendentals=0),
        name="results",
    )(loss, query_grad, table_grad)
    return (loss.reshape(queries), query_grad, table_grad)


def solution(mesh):
    placed = (
        P(("pool", "blk"), None),
        P(("pool", "blk"), None),
        P(),
        P(),
        P(),
        P(("pool", "blk"), None),
        P(("pool", "blk"), None),
        P(("pool", "blk")),
    )
    return jax.shard_map(
        on_device,
        mesh=mesh,
        in_specs=placed,
        out_specs=(P(("pool", "blk")), P(("pool", "blk"), None), P(("pool", "blk"), None)),
        check_vma=False,
    )
```
